256 devices in a mesh: grp: 8 (over z), voc: 32 (over y, x, core).
Axes of the slice: x: 4, y: 4, z: 8, core: 2. Of those that a mesh axis runs over, the one named last changes fastest.
Arguments:
- hidden: bfloat16 [2048, 1280], P(('grp', 'voc')), parts along dimension 0, may hold values from -16 to 16
- head_weight: bfloat16 [1280, 77824], P(None, 'voc'), may hold values from -3 to 3
- teacher_logits: bfloat16 [2048, 77824], P(('grp', 'voc')), parts along dimension 0, may hold values from -18 to 360
- token_ids: int32 [2048], P('grp'), parts along dimension 0, may hold values from 0 to 77823
- teacher_map: int32 [32], replicated, may hold values from 0 to 31, each once
- student_map: int32 [32], replicated, may hold values from 0 to 31, each once
Outputs:
- divergence: float32 [2048], P('grp'), parts along dimension 0
- hidden_grad: bfloat16 [2048, 1280], P(('grp', 'voc')), parts along dimension 0
- weight_grad: bfloat16 [1280, 622592], P(None, ('grp', 'voc')), parts along dimension 1
The draws below stay inside these ranges and needn't reach their ends.
There are 8 independent parts, one for each index of `grp`. The reference program is written for one: setup_inputs(seed, part) draws one part's arguments, and reference() takes and returns one part's arrays. A program takes and returns all parts, laid end to end along the dimension named above; an argument that names none is the same for every part. Nothing has to cross between parts.
Inputs may be any that keep to these rules, and one draw needn't show every extreme that they name: `teacher_map`: a permutation of the 32 blocks. `student_map`: a permutation of the 32 blocks.
All inputs are finite; a program needn't handle non-finite values.
Results may differ from the reference program's by a relative error of at most 0.0053.
Values may be sent and summed in bfloat16 or wider, within the bound.
A program may use at most 64 MiB of HBM per device.

```python
import math
import jax
import jax.numpy as jnp
import numpy as np

D = 1280
VOC_DEV = 2432
VOCAB = 77824
TOKENS = 256
N_VOC = 32


def draw_head_weight(key, part):
    key = jax.random.fold_in(key, 3)
    shared = jax.random.normal(key, (D, VOCAB), jnp.float32) * (3.0 / math.sqrt(D))
    return jnp.clip(shared, -3.0, 3.0).astype(jnp.bfloat16)


def draw_hidden(key, part):
    key = jax.random.fold_in(key, 5)
    values = jax.random.normal(key, (TOKENS, D), jnp.float32)
    return jnp.clip(values, -16.0, 16.0).astype(jnp.bfloat16)


def draw_teacher_logits(key, part):
    key = jax.random.fold_in(key, 7)
    values = jnp.clip(3.0 * jax.random.normal(key, (TOKENS, VOCAB), jnp.float32), -18.0, 18.0)
    return values.astype(jnp.bfloat16)


def set_ends(result, rng, smallest, largest):
    dims = result.shape
    place = [jax.random.randint(jax.random.fold_in(rng, axis), (), 0, dims[axis]) for axis in range(len(dims))]
    result = result.at[tuple(place)].set(smallest)
    longest = dims.index(max(dims))
    place[longest] = (place[longest] + 1) % dims[longest]
    return result.at[tuple(place)].set(largest)


def wide_ids(own_key, shape, number_of, lean):
    portions = [min(1 << octave, number_of + 1 - (1 << octave)) * (1 << 20) // math.isqrt((1 << octave) ** lean) + 1 for octave in range((number_of + 1).bit_length()) if 1 << octave <= number_of]
    spread = 1 + sum(portions) // (1 << 30)
    table = np.cumsum(np.array([max(1, weight // spread) for weight in portions]))
    ticket = jax.random.randint(jax.random.fold_in(own_key, 1), shape, 0, int(table[len(portions) - 1]))
    start = jnp.left_shift(1, jnp.searchsorted(jnp.asarray(table, jnp.int32), ticket, side="right").astype(jnp.int32))
    rank = start - 1 + jax.random.randint(jax.random.fold_in(own_key, 4), shape, 0, 1 << 30) % jnp.minimum(start, number_of + 1 - start)
    return jax.random.permutation(jax.random.fold_in(own_key, 2), number_of)[rank].astype(jnp.int32)


def setup_inputs(seed: int = 0, part: int = 0) -> dict:
    splits = jax.random.split(jax.random.key(seed), 7)
    own_keys = jax.random.split(jax.random.fold_in(splits[6], part), 7)
    hidden = draw_hidden(jax.random.fold_in(jax.random.fold_in(splits[6], part), 71), part)
    head_weight = draw_head_weight(jax.random.fold_in(splits[6], 71), part)
    teacher_logits = draw_teacher_logits(jax.random.fold_in(jax.random.fold_in(splits[6], part), 71), part)
    token_ids = set_ends(wide_ids(own_keys[3], (TOKENS,), VOCAB, 2), jax.random.fold_in(own_keys[3], 3), 0, VOCAB - 1).astype(jnp.int32)
    teacher_map = jax.random.permutation(splits[4], N_VOC).astype(jnp.int32)
    student_map = jax.random.permutation(splits[5], N_VOC).astype(jnp.int32)
    return dict(hidden=hidden, head_weight=head_weight, teacher_logits=teacher_logits, token_ids=token_ids, teacher_map=teacher_map, student_map=student_map)


def reference(hidden, head_weight, teacher_logits, token_ids, teacher_map, student_map):
    blocks = N_VOC
    matches = (teacher_map[:, None] == student_map[None, :]).astype(jnp.int32)
    positions = jnp.sum(matches * jnp.arange(blocks, dtype=jnp.int32)[:, None], axis=0).astype(jnp.int32)
    reordered = jnp.take(teacher_logits.reshape(TOKENS, blocks, VOC_DEV), positions, axis=1)
    teacher = reordered.reshape(TOKENS, VOCAB).astype(jnp.float32)
    logits = jnp.dot(hidden, head_weight, preferred_element_type=jnp.float32)
    log_student = logits - jax.nn.logsumexp(logits, axis=1, keepdims=True)
    log_teacher = teacher - jax.nn.logsumexp(teacher, axis=1, keepdims=True)
    student_prob = jnp.exp(log_student)
    gap = log_student - log_teacher
    divergence = jnp.sum(student_prob * gap, axis=1)
    columns = jnp.arange(VOCAB, dtype=jnp.int32)
    column_ids = (student_map[columns // VOC_DEV] * VOC_DEV + columns % VOC_DEV).astype(jnp.int32)
    onehot = column_ids[None, :] == token_ids[:, None]
    sampled_gap = jnp.sum(jnp.where(onehot, gap, 0.0), axis=1)
    logit_grad = student_prob * (gap - divergence[:, None]) + sampled_gap[:, None] * (onehot.astype(jnp.float32) - student_prob)
    logit_grad = logit_grad.astype(jnp.bfloat16)
    hidden_grad = jax.lax.dot_general(logit_grad, head_weight, (((1,), (1,)), ((), ())), preferred_element_type=jnp.float32)
    weight_grad = jax.lax.dot_general(hidden, logit_grad, (((0,), (0,)), ((), ())), preferred_element_type=jnp.float32)
    return divergence, hidden_grad.astype(jnp.bfloat16), weight_grad.astype(jnp.bfloat16)
```

```python
import functools

import jax
import jax.numpy as jnp
from jax import lax
from jax.experimental import pallas as pl
from jax.experimental.pallas import tpu as pltpu
from jax.sharding import PartitionSpec as P

MESH = pl.DeviceIdType.MESH
F32 = jnp.float32
BF16 = jnp.bfloat16


def tiles(width, size):
    return [(start, min(size, width - start)) for start in range(0, width, size)]


def kernel(
    n,
    hidden_ref,
    head_ref,
    teacher_ref,
    token_ref,
    teacher_map,
    student_map,
    div_ref,
    hgrad_ref,
    wgrad_ref,
    head,
    mine,
    staged,
    teacher,
    gathered,
    hid,
    hid_t,
    diff,
    expo,
    grad,
    tok_col,
    stat,
    stat_out,
    stat_in,
    part_sib,
    part_own,
    pair_in,
    red_out,
    red_in,
    local_sem,
    m_sem,
    t_send,
    t_recv,
    h_send,
    h_recv,
    f_send,
    f_recv,
    s_send,
    s_recv,
    p_send,
    p_recv,
    r_send,
    r_recv,
):
    chips = n // 2
    rows, width = hidden_ref.shape
    block = head_ref.shape[1]
    half = chips * rows
    tokens = 2 * half
    me = lax.axis_index("voc")
    core, chip = me % 2, me // 2
    sibling = me + 1 - 2 * core
    my_block = core * chips + chip

    def slot(device):
        return (device % 2) * chips + device // 2

    def remote(src, dst, send, recv, device):
        return pltpu.make_async_remote_copy(
            src_ref=src, dst_ref=dst, send_sem=send, recv_sem=recv,
            device_id={"voc": device}, device_id_type=MESH,
        )

    barrier = pltpu.get_barrier_semaphore()

    @pl.loop(1, n)
    def _(step):
        pl.semaphore_signal(barrier, inc=1, device_id={"voc": (me + step) % n}, device_id_type=MESH)

    def teacher_in(p):
        return pltpu.make_async_copy(
            teacher_ref.at[:, pl.ds(pl.multiple_of(p * block, 128), block)], mine.at[p], m_sem.at[p]
        )

    @pl.loop(0, n)
    def _(p):
        teacher_in(p).start()

    head_in = pltpu.make_async_copy(head_ref, head, local_sem.at[0])
    head_in.start()

    eye = (
        lax.broadcasted_iota(jnp.int32, (tokens, tokens), 0)
        == lax.broadcasted_iota(jnp.int32, (tokens, tokens), 1)
    )
    ids = jnp.sum(jnp.where(eye, token_ref[...].astype(F32), 0.0), axis=1, keepdims=True)
    ids = ids - (student_map[me] * block).astype(F32)
    ids = jnp.broadcast_to(ids, (tokens, 128)).reshape(chips, 2, rows, 128)
    tok_col[...] = jnp.concatenate([ids[:, 0], ids[:, 1]], axis=0).reshape(tokens, 128)

    gathered[my_block] = hidden_ref[...]

    place = lax.broadcasted_iota(jnp.int32, (1, tokens), 1) // rows
    teacher_id = jnp.zeros((1, tokens), F32)
    student_id = jnp.zeros((1, tokens), F32)
    for p in range(n):
        teacher_id = jnp.where(place == p, teacher_map[p].astype(F32), teacher_id)
        student_id = jnp.where(place == p, student_map[p].astype(F32), student_id)
    wanted = jnp.sum(jnp.where(eye, student_id, 0.0), axis=1, keepdims=True)
    same_row = (
        lax.broadcasted_iota(jnp.int32, (tokens, tokens), 0) % rows
        == lax.broadcasted_iota(jnp.int32, (tokens, tokens), 1) % rows
    )
    move = jnp.where(jnp.logical_and(wanted == teacher_id, same_row), 1.0, 0.0).astype(BF16)

    @pl.loop(0, n)
    def _(p):
        teacher_in(p).wait()

    for start, size in tiles(block, 256):
        piece = mine[:, :, start : start + size].astype(F32).reshape(tokens, size).astype(BF16)
        piece = jnp.dot(move, piece, preferred_element_type=F32)
        staged[:, :, start : start + size] = piece.reshape(n, rows, size).astype(BF16)

    pl.semaphore_wait(barrier, n - 1)

    def hidden_out(other):
        return remote(
            gathered.at[my_block], gathered.at[my_block], h_send.at[other], h_recv.at[chip], other * 2 + core
        )

    def hidden_in(other):
        return remote(
            gathered.at[core * chips + other], gathered.at[core * chips + other],
            h_send.at[other], h_recv.at[other], other * 2 + core,
        )

    def forward(other):
        return remote(
            gathered.at[core * chips + other], gathered.at[core * chips + other],
            f_send.at[other], f_recv.at[other], sibling,
        )

    def forwarded(other):
        return remote(
            gathered.at[(1 - core) * chips + other], gathered.at[(1 - core) * chips + other],
            f_send.at[other], f_recv.at[other], sibling,
        )

    @pl.loop(1, chips)
    def _(step):
        hidden_out((chip + step) % chips).start()

    forward(chip).start()

    def teacher_out(other):
        return remote(staged.at[other], teacher.at[me], t_send.at[other], t_recv.at[me], other)

    def teacher_from(other):
        return remote(staged.at[other], teacher.at[other], t_send.at[other], t_recv.at[other], other)

    @pl.loop(1, n)
    def _(step):
        teacher_out((me + step) % n).start()

    teacher[me] = staged[me]

    top = jnp.full((rows, 128), -jnp.inf, F32)
    top = lax.fori_loop(
        0, n,
        lambda j, top: functools.reduce(
            jnp.maximum,
            [staged[j, :, pl.ds(c, 128)].astype(F32) for c in range(0, block, 128)], top),
        top,
    )
    top = jnp.max(top, axis=1, keepdims=True)
    total = lax.fori_loop(
        0, n,
        lambda j, total: functools.reduce(
            jnp.add,
            [jnp.exp(staged[j, :, pl.ds(c, 128)].astype(F32) - top) for c in range(0, block, 128)], total),
        jnp.zeros((rows, 128), F32),
    )
    norm_mine = top + jnp.log(jnp.sum(total, axis=1, keepdims=True))

    @pl.loop(1, chips)
    def _(step):
        other = (chip + chips - step) % chips
        hidden_in(other).wait_recv()
        forward(other).start()

    def unpack(which):
        base = pl.multiple_of(which * half, half)
        flat = gathered[pl.ds(pl.multiple_of(which * chips, chips), chips)].astype(F32).reshape(half, width)
        hid[pl.ds(base, half), :] = flat.astype(BF16)
        hid_t[:, pl.ds(base, half)] = flat.T.astype(BF16)

    unpack(core)

    @pl.loop(0, chips)
    def _(other):
        forwarded(other).wait_recv()

    unpack(1 - core)
    head_in.wait()

    for start, size in tiles(block, 512):
        diff[:, start : start + size] = jnp.dot(
            hid[...], head[:, start : start + size], preferred_element_type=F32
        )

    lane = lax.broadcasted_iota(jnp.int32, (rows, 128), 1)

    @pl.loop(0, n)
    def _(b):
        at = pl.ds(pl.multiple_of(b * rows, rows), rows)
        logits = diff[at, :]
        peak = jnp.max(logits, axis=1, keepdims=True)
        e = jnp.exp(logits - peak)
        expo[at, :] = e
        mass = jnp.sum(e, axis=1, keepdims=True)
        stat[at, :] = jnp.where(lane == 0, peak, jnp.where(lane == 1, mass, 0.0))

    at = pl.ds(pl.multiple_of(my_block * rows, rows), rows)
    stat[at, :] = jnp.where(lane == 4, norm_mine, stat[at, :])

    column = lax.broadcasted_iota(jnp.int32, (rows, block), 1).astype(F32)

    @pl.loop(0, n)
    def _(step):
        other = (me + n - step) % n

        @pl.when(step > 0)
        def _():
            teacher_from(other).wait_recv()

        at = pl.ds(pl.multiple_of(slot(other) * rows, rows), rows)
        u = diff[at, :] - teacher[other].astype(F32)
        diff[at, :] = u
        cross = jnp.sum(expo[at, :] * u, axis=1, keepdims=True)
        hit = jnp.sum(jnp.where(column == tok_col[at, 0:1], u, 0.0), axis=1, keepdims=True)
        stat[at, :] = jnp.where(lane == 2, cross, jnp.where(lane == 3, hit, stat[at, :]))

    own = stat[...].T[0:8, :]
    stat_out[...] = own
    stat_in[me] = own

    def stat_to(other):
        return remote(stat_out, stat_in.at[me], s_send.at[other], s_recv.at[me], other)

    def stat_from(other):
        return remote(stat_out, stat_in.at[other], s_send.at[other], s_recv.at[other], other)

    @pl.loop(1, n)
    def _(step):
        stat_to((me + step) % n).start()

    @pl.loop(1, n)
    def _(step):
        stat_from((me + n - step) % n).wait_recv()

    peak = functools.reduce(jnp.maximum, [stat_in[d] for d in range(n)])[0:1, :]
    row = lax.broadcasted_iota(jnp.int32, (8, tokens), 0)
    weighted = jnp.logical_or(row == 1, row == 2)
    total = jnp.zeros((8, tokens), F32)
    for d in range(n):
        block_stat = stat_in[d]
        total = total + jnp.where(weighted, jnp.exp(block_stat[0:1, :] - peak), 1.0) * block_stat
    mass, cross, hit, norm_teacher = (total[i : i + 1, :] for i in range(1, 5))
    norm_student = peak + jnp.log(mass)
    mean = cross / mass
    sampled = hit - norm_student + norm_teacher
    div = mean - norm_student + norm_teacher
    scale = jnp.exp(own[0:1, :] - norm_student)
    shift = mean + sampled
    final = jnp.where(
        row == 0, scale, jnp.where(row == 1, shift, jnp.where(row == 2, sampled, jnp.where(row == 3, div, 0.0)))
    )
    columns = jnp.concatenate([final, jnp.zeros((120, tokens), F32)], axis=0).T
    stat[...] = columns
    halves = columns.reshape(2, chips, rows, 128)
    ordered = jnp.stack([halves[0], halves[1]], axis=1).reshape(tokens, 128)
    div_ref[...] = ordered.T[3:4, :]

    wide = lax.broadcasted_iota(jnp.int32, (2 * rows, block), 1).astype(F32)

    @pl.loop(0, n // 2)
    def _(b):
        at = pl.ds(pl.multiple_of(b * 2 * rows, 2 * rows), 2 * rows)
        g = expo[at, :] * (stat[at, 0:1] * (diff[at, :] - stat[at, 1:2]))
        g = g + jnp.where(wide == tok_col[at, 0:1], stat[at, 2:3], 0.0)
        grad[at, :] = g.astype(BF16)

    own_rows = pl.ds(pl.multiple_of(core * half, half), half)
    sib_rows = pl.ds(pl.multiple_of((1 - core) * half, half), half)
    pieces = tiles(width, 256)

    def pair(i):
        return remote(part_sib.at[i], pair_in.at[i], p_send.at[i], p_recv.at[i], sibling)

    for i, (start, size) in enumerate(pieces):
        part = lax.dot_general(
            grad[...], head[start : start + size, :], (((1,), (1,)), ((), ())), preferred_element_type=F32
        )
        stat_rows = jnp.where(core == 0, part[half:], part[:half])
        part_sib[i] = stat_rows
        part_own[i] = jnp.where(core == 0, part[:half], part[half:])
        pair(i).start()

    for i, (start, size) in enumerate(pieces):
        pair(i).wait_recv()
        total = part_own[i] + pair_in[i]
        part_own[i] = total
        red_out[:, :, start : start + size] = total.reshape(chips, rows, size).astype(BF16)

    def reduce_to(other):
        return remote(red_out.at[other], red_in.at[chip], r_send.at[other], r_recv.at[chip], other * 2 + core)

    def reduce_from(other):
        return remote(red_out.at[other], red_in.at[other], r_send.at[other], r_recv.at[other], other * 2 + core)

    @pl.loop(1, chips)
    def _(step):
        reduce_to((chip + step) % chips).start()

    red_in[chip] = jnp.zeros((rows, width), BF16)

    for start, size in tiles(block, 256):
        wgrad_ref[:, start : start + size] = jnp.dot(
            hid_t[...], grad[:, start : start + size], preferred_element_type=F32
        ).astype(BF16)

    @pl.loop(1, chips)
    def _(step):
        reduce_from((chip + chips - step) % chips).wait_recv()

    at = pl.ds(pl.multiple_of(chip * rows, rows), rows)
    for i, (start, size) in enumerate(pieces):
        total = part_own[i, at, :]
        for k in range(chips):
            total = total + red_in[k, :, start : start + size].astype(F32)
        hgrad_ref[:, start : start + size] = total.astype(BF16)

    @pl.loop(1, chips)
    def _(step):
        other = (chip + step) % chips
        hidden_out(other).wait_send()
        reduce_to(other).wait_send()

    @pl.loop(0, chips)
    def _(other):
        forward(other).wait_send()

    @pl.loop(1, n)
    def _(step):
        other = (me + step) % n
        teacher_out(other).wait_send()
        stat_to(other).wait_send()

    for i in range(len(pieces)):
        pair(i).wait_send()


def on_device(hidden, head_weight, teacher_logits, token_ids, teacher_map, student_map):
    n = lax.axis_size("voc")
    chips = n // 2
    rows, width = hidden.shape
    block = head_weight.shape[1]
    tokens = n * rows
    half = chips * rows
    pieces = len(tiles(width, 256))
    dma = pltpu.SemaphoreType.DMA
    vmem = pl.BlockSpec(memory_space=pltpu.VMEM)
    smem = pl.BlockSpec(memory_space=pltpu.SMEM)
    hbm = pl.BlockSpec(memory_space=pl.ANY)
    div, hgrad, wgrad = pl.pallas_call(
        functools.partial(kernel, n),
        out_shape=(
            jax.ShapeDtypeStruct((1, tokens), F32),
            jax.ShapeDtypeStruct((rows, width), BF16),
            pltpu.VMEM((width, block), BF16),
        ),
        in_specs=[vmem, hbm, hbm, vmem, smem, smem],
        out_specs=(vmem, vmem, vmem),
        scratch_shapes=[
            pltpu.VMEM((width, block), BF16),
            pltpu.VMEM((n, rows, block), BF16),
            pltpu.VMEM((n, rows, block), BF16),
            pltpu.VMEM((n, rows, block), BF16),
            pltpu.VMEM((n, rows, width), BF16),
            pltpu.VMEM((tokens, width), BF16),
            pltpu.VMEM((width, tokens), BF16),
            pltpu.VMEM((tokens, block), F32),
            pltpu.VMEM((tokens, block), F32),
            pltpu.VMEM((tokens, block), BF16),
            pltpu.VMEM((tokens, 128), F32),
            pltpu.VMEM((tokens, 128), F32),
            pltpu.VMEM((8, tokens), F32),
            pltpu.VMEM((n, 8, tokens), F32),
            pltpu.VMEM((pieces, half, 256), F32),
            pltpu.VMEM((pieces, half, 256), F32),
            pltpu.VMEM((pieces, half, 256), F32),
            pltpu.VMEM((chips, rows, width), BF16),
            pltpu.VMEM((chips, rows, width), BF16),
            dma((1,)),
            dma((n,)),
            dma((n,)),
            dma((n,)),
            dma((chips,)),
            dma((chips,)),
            dma((chips,)),
            dma((chips,)),
            dma((n,)),
            dma((n,)),
            dma((pieces,)),
            dma((pieces,)),
            dma((chips,)),
            dma((chips,)),
        ],
        compiler_params=pltpu.CompilerParams(
            collective_id=0, has_side_effects=True, vmem_limit_bytes=48 * 1024 * 1024
        ),
    )(hidden, head_weight, teacher_logits, token_ids.reshape(1, tokens), teacher_map, student_map)
    return div.reshape(tokens), hgrad, wgrad


def solution(mesh):
    return jax.shard_map(
        on_device,
        mesh=mesh,
        in_specs=(
            P(("grp", "voc"), None),
            P(None, "voc"),
            P(("grp", "voc"), None),
            P("grp"),
            P(),
            P(),
        ),
        out_specs=(P("grp"), P(("grp", "voc"), None), P(None, ("grp", "voc"))),
        check_vma=False,
    )
```

```python
import functools

import jax
import jax.numpy as jnp
from jax import lax
from jax.experimental import pallas as pl
from jax.experimental.pallas import tpu as pltpu
from jax.sharding import PartitionSpec as P

MESH = pl.DeviceIdType.MESH
F32 = jnp.float32
BF16 = jnp.bfloat16


def tiles(width, size):
    return [(start, min(size, width - start)) for start in range(0, width, size)]


def kernel(
    n,
    hidden_ref,
    head_ref,
    teacher_ref,
    token_hbm,
    teacher_map_hbm,
    student_map_hbm,
    div_ref,
    hgrad_ref,
    wgrad_ref,
    token_ref,
    teacher_map,
    student_map,
    head,
    mine,
    staged,
    teacher,
    gathered,
    hid,
    hid_t,
    grad,
    diff,
    expo,
    tok_col,
    stat,
    peaks,
    masses,
    norms,
    crosses,
    hits,
    stat_out,
    stat_in,
    part_sib,
    part_own,
    pair_in,
    red_out,
    red_in,
    local_sem,
    m_sem,
    t_send,
    t_recv,
    h_send,
    h_recv,
    f_send,
    f_recv,
    s_send,
    s_recv,
    p_send,
    p_recv,
    r_send,
    r_recv,
):
    chips = n // 2
    rows, width = hidden_ref.shape
    block = head_ref.shape[1]
    half = chips * rows
    tokens = 2 * half
    me = lax.axis_index("voc")
    core, chip = me % 2, me // 2
    sibling = me + 1 - 2 * core
    my_block = core * chips + chip

    def slot(device):
        return (device % 2) * chips + device // 2

    def remote(src, dst, send, recv, device):
        return pltpu.make_async_remote_copy(
            src_ref=src, dst_ref=dst, send_sem=send, recv_sem=recv,
            device_id={"voc": device}, device_id_type=MESH,
        )

    barrier = pltpu.get_barrier_semaphore()

    @pl.loop(1, n)
    def _(step):
        pl.semaphore_signal(barrier, inc=1, device_id={"voc": (me + step) % n}, device_id_type=MESH)

    small = [
        pltpu.make_async_copy(token_hbm, token_ref, local_sem.at[1]),
        pltpu.make_async_copy(teacher_map_hbm, teacher_map, local_sem.at[2]),
        pltpu.make_async_copy(student_map_hbm, student_map, local_sem.at[3]),
        pltpu.make_async_copy(hidden_ref, gathered.at[my_block], local_sem.at[4]),
    ]
    for copy in small:
        copy.start()

    def teacher_in(p):
        return pltpu.make_async_copy(
            teacher_ref.at[:, pl.ds(pl.multiple_of(p * block, 128), block)], mine.at[p], m_sem.at[p]
        )

    @pl.loop(0, n)
    def _(p):
        teacher_in(p).start()

    head_in = pltpu.make_async_copy(head_ref, head, local_sem.at[0])
    head_in.start()

    for copy in small:
        copy.wait()

    eye = (
        lax.broadcasted_iota(jnp.int32, (tokens, tokens), 0)
        == lax.broadcasted_iota(jnp.int32, (tokens, tokens), 1)
    )
    ids = jnp.sum(jnp.where(eye, token_ref[...].astype(F32), 0.0), axis=1, keepdims=True)
    ids = ids - (student_map[me] * block).astype(F32)
    ids = jnp.broadcast_to(ids, (tokens, 128)).reshape(chips, 2, rows, 128)
    tok_col[...] = jnp.concatenate([ids[:, 0], ids[:, 1]], axis=0).reshape(tokens, 128)

    place = lax.broadcasted_iota(jnp.int32, (1, tokens), 1) // rows
    teacher_id = jnp.zeros((1, tokens), F32)
    student_id = jnp.zeros((1, tokens), F32)
    for p in range(n):
        teacher_id = jnp.where(place == p, teacher_map[p].astype(F32), teacher_id)
        student_id = jnp.where(place == p, student_map[p].astype(F32), student_id)
    wanted = jnp.sum(jnp.where(eye, student_id, 0.0), axis=1, keepdims=True)
    same_row = (
        lax.broadcasted_iota(jnp.int32, (tokens, tokens), 0) % rows
        == lax.broadcasted_iota(jnp.int32, (tokens, tokens), 1) % rows
    )
    move = jnp.where(jnp.logical_and(wanted == teacher_id, same_row), 1.0, 0.0).astype(BF16)

    @pl.loop(0, n)
    def _(p):
        teacher_in(p).wait()

    for start, size in tiles(block, 256):
        piece = mine[:, :, start : start + size].astype(F32).reshape(tokens, size).astype(BF16)
        piece = jnp.dot(move, piece, preferred_element_type=F32)
        staged[:, :, start : start + size] = piece.reshape(n, rows, size).astype(BF16)

    pl.semaphore_wait(barrier, n - 1)

    def hidden_out(other):
        return remote(
            gathered.at[my_block], gathered.at[my_block], h_send.at[other], h_recv.at[chip], other * 2 + core
        )

    def hidden_in(other):
        return remote(
            gathered.at[core * chips + other], gathered.at[core * chips + other],
            h_send.at[other], h_recv.at[other], other * 2 + core,
        )

    def forward(other):
        return remote(
            gathered.at[core * chips + other], gathered.at[core * chips + other],
            f_send.at[other], f_recv.at[other], sibling,
        )

    def forwarded(other):
        return remote(
            gathered.at[(1 - core) * chips + other], gathered.at[(1 - core) * chips + other],
            f_send.at[other], f_recv.at[other], sibling,
        )

    @pl.loop(1, chips)
    def _(step):
        hidden_out((chip + step) % chips).start()

    forward(chip).start()

    def teacher_out(other):
        return remote(staged.at[other], teacher.at[me], t_send.at[other], t_recv.at[me], other)

    def teacher_from(other):
        return remote(staged.at[other], teacher.at[other], t_send.at[other], t_recv.at[other], other)

    @pl.loop(1, n)
    def _(step):
        teacher_out((me + step) % n).start()

    teacher[me] = staged[me]

    spots = [c for c, _ in tiles(block, 128)]

    def spread(op, values, carry):
        carry = list(carry)
        for i, value in enumerate(values):
            carry[i % 4] = op(carry[i % 4], value)
        return tuple(carry)

    def gather4(op, carry):
        return op(op(carry[0], carry[1]), op(carry[2], carry[3]))

    top = lax.fori_loop(
        0, n,
        lambda j, carry: spread(jnp.maximum, [staged[j, :, c : c + 128].astype(F32) for c in spots], carry),
        (jnp.full((rows, 128), -jnp.inf, F32),) * 4,
    )
    top = jnp.max(gather4(jnp.maximum, top), axis=1, keepdims=True)
    total = lax.fori_loop(
        0, n,
        lambda j, carry: spread(
            jnp.add, [jnp.exp(staged[j, :, c : c + 128].astype(F32) - top) for c in spots], carry
        ),
        (jnp.zeros((rows, 128), F32),) * 4,
    )
    norm_mine = top + jnp.log(jnp.sum(gather4(jnp.add, total), axis=1, keepdims=True))

    @pl.loop(1, chips)
    def _(step):
        other = (chip + chips - step) % chips
        hidden_in(other).wait_recv()
        forward(other).start()

    def unpack(which):
        base = pl.multiple_of(which * half, half)
        flat = gathered[pl.ds(pl.multiple_of(which * chips, chips), chips)].astype(F32).reshape(half, width)
        hid[pl.ds(base, half), :] = flat.astype(BF16)
        hid_t[:, pl.ds(base, half)] = flat.T.astype(BF16)

    unpack(core)

    @pl.loop(0, chips)
    def _(other):
        forwarded(other).wait_recv()

    unpack(1 - core)
    head_in.wait()

    for start, size in tiles(block, 512):
        diff[:, start : start + size] = jnp.dot(
            hid[...], head[:, start : start + size], preferred_element_type=F32
        )

    group = 64

    @pl.loop(0, tokens // group)
    def _(b):
        at = pl.ds(pl.multiple_of(b * group, group), group)
        top = diff[at, 0:128]
        for c in spots[1:]:
            top = jnp.maximum(top, diff[at, c : c + 128])
        top = jnp.broadcast_to(jnp.max(top, axis=1, keepdims=True), (group, 128))
        peaks[at, :] = top
        total = jnp.zeros((group, 128), F32)
        for c in spots:
            e = jnp.exp(diff[at, c : c + 128] - top)
            expo[at, c : c + 128] = e
            total = total + e
        masses[at, :] = total

    norms[...] = jnp.zeros_like(norms)
    norms[pl.ds(pl.multiple_of(my_block * rows, rows), rows), :] = jnp.broadcast_to(norm_mine, (rows, 128))
    early = [
        peaks[...].T[0:1, :],
        jnp.sum(masses[...].T, axis=0, keepdims=True),
        norms[...].T[0:1, :],
    ]
    lane = lax.broadcasted_iota(jnp.int32, (rows, 128), 1).astype(F32)

    @pl.loop(0, n)
    def _(step):
        other = (me + n - step) % n

        @pl.when(step > 0)
        def _():
            teacher_from(other).wait_recv()

        at = pl.ds(pl.multiple_of(slot(other) * rows, rows), rows)
        picked = tok_col[at, :] - lane
        cross = [jnp.zeros((rows, 128), F32)] * 4
        hit = [jnp.zeros((rows, 128), F32)] * 4
        for i, c in enumerate(spots):
            u = diff[at, c : c + 128] - teacher[other, :, c : c + 128].astype(F32)
            diff[at, c : c + 128] = u
            cross[i % 4] = cross[i % 4] + expo[at, c : c + 128] * u
            hit[i % 4] = hit[i % 4] + jnp.where(picked == float(c), u, 0.0)
        crosses[at, :] = gather4(jnp.add, cross)
        hits[at, :] = gather4(jnp.add, hit)

    row = lax.broadcasted_iota(jnp.int32, (8, tokens), 0)

    def rows_of(values):
        out = jnp.zeros((8, tokens), F32)
        for i, value in enumerate(values):
            out = jnp.where(row == i, value, out)
        return out

    own = rows_of([
        early[0], early[1],
        jnp.sum(crosses[...].T, axis=0, keepdims=True),
        jnp.sum(hits[...].T, axis=0, keepdims=True),
        early[2],
    ])
    stat_out[...] = own
    stat_in[me] = own

    def stat_to(other):
        return remote(stat_out, stat_in.at[me], s_send.at[other], s_recv.at[me], other)

    def stat_from(other):
        return remote(stat_out, stat_in.at[other], s_send.at[other], s_recv.at[other], other)

    @pl.loop(1, n)
    def _(step):
        stat_to((me + step) % n).start()

    @pl.loop(1, n)
    def _(step):
        stat_from((me + n - step) % n).wait_recv()

    peak = functools.reduce(jnp.maximum, [stat_in[d] for d in range(n)])[0:1, :]
    weighted = jnp.logical_or(row == 1, row == 2)
    total = jnp.zeros((8, tokens), F32)
    for d in range(n):
        block_stat = stat_in[d]
        total = total + jnp.where(weighted, jnp.exp(block_stat[0:1, :] - peak), 1.0) * block_stat
    mass, cross, hit, norm_teacher = (total[i : i + 1, :] for i in range(1, 5))
    norm_student = peak + jnp.log(mass)
    mean = cross / mass
    sampled = hit - norm_student + norm_teacher
    div = mean - norm_student + norm_teacher
    scale = jnp.exp(own[0:1, :] - norm_student)
    shift = mean + sampled
    final = rows_of([scale, shift, sampled, div])
    columns = jnp.concatenate([final, jnp.zeros((120, tokens), F32)], axis=0).T
    stat[...] = columns
    halves = columns.reshape(2, chips, rows, 128)
    ordered = jnp.stack([halves[0], halves[1]], axis=1).reshape(tokens, 128)
    div_ref[...] = ordered.T[3:4, :]

    span = 32

    @pl.loop(0, tokens // span)
    def _(b):
        at = pl.ds(pl.multiple_of(b * span, span), span)
        wide = lax.broadcasted_iota(jnp.int32, (span, 128), 1).astype(F32)
        picked = tok_col[at, :] - wide
        scale = jnp.broadcast_to(stat[at, 0:1], (span, 128))
        shift = jnp.broadcast_to(stat[at, 1:2], (span, 128))
        sampled = jnp.broadcast_to(stat[at, 2:3], (span, 128))
        for c in spots:
            g = expo[at, c : c + 128] * (scale * (diff[at, c : c + 128] - shift))
            g = g + jnp.where(picked == float(c), sampled, 0.0)
            grad[at, c : c + 128] = g.astype(BF16)

    own_rows = pl.ds(pl.multiple_of(core * half, half), half)
    sib_rows = pl.ds(pl.multiple_of((1 - core) * half, half), half)
    pieces = tiles(width, 256)

    def pair(i):
        return remote(part_sib.at[i], pair_in.at[i], p_send.at[i], p_recv.at[i], sibling)

    for i, (start, size) in enumerate(pieces):
        part = lax.dot_general(
            grad[...], head[start : start + size, :], (((1,), (1,)), ((), ())), preferred_element_type=F32
        )
        stat_rows = jnp.where(core == 0, part[half:], part[:half])
        part_sib[i] = stat_rows
        part_own[i] = jnp.where(core == 0, part[:half], part[half:])
        pair(i).start()

    for i, (start, size) in enumerate(pieces):
        pair(i).wait_recv()
        total = part_own[i] + pair_in[i]
        part_own[i] = total
        red_out[:, :, start : start + size] = total.reshape(chips, rows, size).astype(BF16)

    def reduce_to(other):
        return remote(red_out.at[other], red_in.at[chip], r_send.at[other], r_recv.at[chip], other * 2 + core)

    def reduce_from(other):
        return remote(red_out.at[other], red_in.at[other], r_send.at[other], r_recv.at[other], other * 2 + core)

    @pl.loop(1, chips)
    def _(step):
        reduce_to((chip + step) % chips).start()

    red_in[chip] = jnp.zeros((rows, width), BF16)

    for start, size in tiles(block, 256):
        wgrad_ref[:, start : start + size] = jnp.dot(
            hid_t[...], grad[:, start : start + size], preferred_element_type=F32
        ).astype(BF16)

    @pl.loop(1, chips)
    def _(step):
        reduce_from((chip + chips - step) % chips).wait_recv()

    at = pl.ds(pl.multiple_of(chip * rows, rows), rows)
    for i, (start, size) in enumerate(pieces):
        total = part_own[i, at, :]
        for k in range(chips):
            total = total + red_in[k, :, start : start + size].astype(F32)
        hgrad_ref[:, start : start + size] = total.astype(BF16)

    @pl.loop(1, chips)
    def _(step):
        other = (chip + step) % chips
        hidden_out(other).wait_send()
        reduce_to(other).wait_send()

    @pl.loop(0, chips)
    def _(other):
        forward(other).wait_send()

    @pl.loop(1, n)
    def _(step):
        other = (me + step) % n
        teacher_out(other).wait_send()
        stat_to(other).wait_send()

    for i in range(len(pieces)):
        pair(i).wait_send()


def out_kernel(div, hgrad, wgrad, div_out, hgrad_out, wgrad_out, sem):
    strip = wgrad.shape[0] // 8
    copies = [
        pltpu.make_async_copy(wgrad.at[pl.ds(i * strip, strip)], wgrad_out.at[pl.ds(i * strip, strip)], sem.at[i])
        for i in range(8)
    ]
    copies.append(pltpu.make_async_copy(div, div_out, sem.at[8]))
    copies.append(pltpu.make_async_copy(hgrad, hgrad_out, sem.at[9]))
    for copy in copies:
        copy.start()
    for copy in copies:
        copy.wait()


def on_device(hidden, head_weight, teacher_logits, token_ids, teacher_map, student_map):
    n = lax.axis_size("voc")
    chips = n // 2
    rows, width = hidden.shape
    block = head_weight.shape[1]
    tokens = n * rows
    half = chips * rows
    pieces = len(tiles(width, 256))
    dma = pltpu.SemaphoreType.DMA
    vmem = pl.BlockSpec(memory_space=pltpu.VMEM)
    hbm = pl.BlockSpec(memory_space=pltpu.HBM)
    div, hgrad, wgrad = pl.pallas_call(
        functools.partial(kernel, n),
        out_shape=(
            pltpu.VMEM((1, tokens), F32),
            pltpu.VMEM((rows, width), BF16),
            pltpu.VMEM((width, block), BF16),
        ),
        in_specs=[hbm] * 6,
        out_specs=(vmem, vmem, vmem),
        scratch_shapes=[
            pltpu.VMEM((1, tokens), jnp.int32),
            pltpu.SMEM((n,), jnp.int32),
            pltpu.SMEM((n,), jnp.int32),
            pltpu.VMEM((width, block), BF16),
            pltpu.VMEM((n, rows, block), BF16),
            pltpu.VMEM((n, rows, block), BF16),
            pltpu.VMEM((n, rows, block), BF16),
            pltpu.VMEM((n, rows, width), BF16),
            pltpu.VMEM((tokens, width), BF16),
            pltpu.VMEM((width, tokens), BF16),
            pltpu.VMEM((tokens, block), BF16),
            pltpu.VMEM((tokens, block), F32),
            pltpu.VMEM((tokens, block), F32),
            pltpu.VMEM((tokens, 128), F32),
            pltpu.VMEM((tokens, 128), F32),
            pltpu.VMEM((tokens, 128), F32),
            pltpu.VMEM((tokens, 128), F32),
            pltpu.VMEM((tokens, 128), F32),
            pltpu.VMEM((tokens, 128), F32),
            pltpu.VMEM((tokens, 128), F32),
            pltpu.VMEM((8, tokens), F32),
            pltpu.VMEM((n, 8, tokens), F32),
            pltpu.VMEM((pieces, half, 256), F32),
            pltpu.VMEM((pieces, half, 256), F32),
            pltpu.VMEM((pieces, half, 256), F32),
            pltpu.VMEM((chips, rows, width), BF16),
            pltpu.VMEM((chips, rows, width), BF16),
            dma((5,)),
            dma((n,)),
            dma((n,)),
            dma((n,)),
            dma((chips,)),
            dma((chips,)),
            dma((chips,)),
            dma((chips,)),
            dma((n,)),
            dma((n,)),
            dma((pieces,)),
            dma((pieces,)),
            dma((chips,)),
            dma((chips,)),
        ],
        compiler_params=pltpu.CompilerParams(
            collective_id=0, has_side_effects=True, vmem_limit_bytes=48 * 1024 * 1024
        ),
    )(*(
        pltpu.with_memory_space_constraint(x, pltpu.HBM)
        for x in (hidden, head_weight, teacher_logits, token_ids.reshape(1, tokens), teacher_map, student_map)
    ))
    div, hgrad, wgrad = pl.pallas_call(
        out_kernel,
        out_shape=(
            jax.ShapeDtypeStruct((1, tokens), F32),
            jax.ShapeDtypeStruct((rows, width), BF16),
            jax.ShapeDtypeStruct((width, block), BF16),
        ),
        in_specs=[vmem] * 3,
        out_specs=(hbm,) * 3,
        scratch_shapes=[dma((10,))],
        compiler_params=pltpu.CompilerParams(vmem_limit_bytes=2 * 1024 * 1024),
    )(*(pltpu.with_memory_space_constraint(x, pltpu.VMEM) for x in (div, hgrad, wgrad)))
    return div.reshape(tokens), hgrad, wgrad


def solution(mesh):
    return jax.shard_map(
        on_device,
        mesh=mesh,
        in_specs=(
            P(("grp", "voc"), None),
            P(None, "voc"),
            P(("grp", "voc"), None),
            P("grp"),
            P(),
            P(),
        ),
        out_specs=(P("grp"), P(("grp", "voc"), None), P(None, ("grp", "voc"))),
        check_vma=False,
    )
```

```python
import functools
import math

import jax
import jax.numpy as jnp
from jax import lax
from jax.experimental import pallas as pl
from jax.experimental.pallas import tpu as pltpu
from jax.sharding import PartitionSpec as P

MESH = pl.DeviceIdType.MESH
F32 = jnp.float32
BF16 = jnp.bfloat16


def tiles(width, size):
    return [(start, min(size, width - start)) for start in range(0, width, size)]


def kernel(
    n,
    hidden_ref,
    head_ref,
    teacher_ref,
    token_hbm,
    teacher_map_hbm,
    student_map_hbm,
    div_ref,
    hgrad_ref,
    wgrad_ref,
    token_ref,
    teacher_map,
    student_map,
    head,
    mine,
    staged,
    teacher,
    gathered,
    hid,
    hid_t,
    grad,
    diff,
    expo,
    tok_col,
    stat,
    peaks,
    masses,
    norms,
    crosses,
    hits,
    stat_out,
    stat_in,
    part_sib,
    part_own,
    pair_in,
    red_out,
    red_in,
    local_sem,
    m_sem,
    t_send,
    t_recv,
    h_send,
    h_recv,
    f_send,
    f_recv,
    s_send,
    s_recv,
    p_send,
    p_recv,
    r_send,
    r_recv,
):
    chips = n // 2
    rows, width = hidden_ref.shape
    block = head_ref.shape[1]
    half = chips * rows
    tokens = 2 * half
    side = math.isqrt(chips)
    me = lax.axis_index("voc")
    core, chip = lax.rem(me, 2), lax.div(me, 2)
    y, x = lax.div(chip, side), lax.rem(chip, side)
    sibling = me + 1 - 2 * core
    my_block = core * chips + chip

    ys = [lax.rem(y + d, side) * side for d in range(side)]
    xs = [lax.rem(x + d, side) for d in range(side)]

    def far(d):
        return -sum(min(v, side - v) for v in d[:2])

    def back(d):
        return (-d[0] % side, -d[1] % side) + d[2:]

    chip_deltas = sorted([(dy, dx) for dy in range(side) for dx in range(side) if dy or dx], key=far)
    device_deltas = sorted([d + (c,) for d in chip_deltas + [(0, 0)] for c in (0, 1)][:-2], key=far) + [(0, 0, 1)]
    cores = [core, 1 - core]

    def chip_at(d):
        return ys[d[0]] + xs[d[1]]

    def device_at(d):
        return chip_at(d) * 2 + cores[d[2]]

    chip_to = [chip_at(d) for d in chip_deltas]
    chip_from = [chip_at(back(d)) for d in chip_deltas]
    device_to = [device_at(d) for d in device_deltas]
    device_from = [device_at(back(d)) for d in device_deltas]

    def remote(src, dst, send, recv, device):
        return pltpu.make_async_remote_copy(
            src_ref=src, dst_ref=dst, send_sem=send, recv_sem=recv,
            device_id={"voc": device}, device_id_type=MESH,
        )

    barrier = pltpu.get_barrier_semaphore()

    for other in device_to:
        pl.semaphore_signal(barrier, inc=1, device_id={"voc": other}, device_id_type=MESH)

    small = [
        pltpu.make_async_copy(token_hbm, token_ref, local_sem.at[1]),
        pltpu.make_async_copy(teacher_map_hbm, teacher_map, local_sem.at[2]),
        pltpu.make_async_copy(student_map_hbm, student_map, local_sem.at[3]),
        pltpu.make_async_copy(hidden_ref, gathered.at[my_block], local_sem.at[4]),
    ]
    for copy in small:
        copy.start()

    def teacher_in(p):
        return pltpu.make_async_copy(
            teacher_ref.at[:, pl.ds(pl.multiple_of(p * block, 128), block)], mine.at[p], m_sem.at[p]
        )

    @pl.loop(0, n)
    def _(p):
        teacher_in(p).start()

    head_in = pltpu.make_async_copy(head_ref, head, local_sem.at[0])
    head_in.start()

    for copy in small:
        copy.wait()

    eye = (
        lax.broadcasted_iota(jnp.int32, (tokens, tokens), 0)
        == lax.broadcasted_iota(jnp.int32, (tokens, tokens), 1)
    )
    ids = jnp.sum(jnp.where(eye, token_ref[...].astype(F32), 0.0), axis=1, keepdims=True)
    ids = ids - (student_map[me] * block).astype(F32)
    ids = jnp.broadcast_to(ids, (tokens, 128)).reshape(chips, 2, rows, 128)
    tok_col[...] = jnp.concatenate([ids[:, 0], ids[:, 1]], axis=0).reshape(tokens, 128)

    place = lax.broadcasted_iota(jnp.int32, (1, tokens), 1) // rows
    teacher_id = jnp.zeros((1, tokens), F32)
    student_id = jnp.zeros((1, tokens), F32)
    for p in range(n):
        teacher_id = jnp.where(place == p, teacher_map[p].astype(F32), teacher_id)
        student_id = jnp.where(place == p, student_map[p].astype(F32), student_id)
    wanted = jnp.sum(jnp.where(eye, student_id, 0.0), axis=1, keepdims=True)
    same_row = (
        lax.broadcasted_iota(jnp.int32, (tokens, tokens), 0) % rows
        == lax.broadcasted_iota(jnp.int32, (tokens, tokens), 1) % rows
    )
    move = jnp.where(jnp.logical_and(wanted == teacher_id, same_row), 1.0, 0.0).astype(BF16)

    @pl.loop(0, n)
    def _(p):
        teacher_in(p).wait()

    for start, size in tiles(block, 256):
        piece = mine[:, :, start : start + size].astype(F32).reshape(tokens, size).astype(BF16)
        piece = jnp.dot(move, piece, preferred_element_type=F32)
        staged[:, :, start : start + size] = piece.reshape(n, rows, size).astype(BF16)

    pl.semaphore_wait(barrier, n - 1)

    def hidden_out(i):
        return remote(
            gathered.at[my_block], gathered.at[my_block], h_send.at[i], h_recv.at[i], chip_to[i] * 2 + core
        )

    def hidden_in(i):
        landed = gathered.at[core * chips + chip_from[i]]
        return remote(landed, landed, h_send.at[i], h_recv.at[i], chip_to[i] * 2 + core)

    def forward(i):
        landed = gathered.at[my_block if i == chips - 1 else core * chips + chip_from[i]]
        return remote(landed, landed, f_send.at[i], f_recv.at[i], sibling)

    def forwarded(i):
        landed = gathered.at[(1 - core) * chips + (chip if i == chips - 1 else chip_from[i])]
        return remote(landed, landed, f_send.at[i], f_recv.at[i], sibling)

    for i in range(chips - 1):
        hidden_out(i).start()
    forward(chips - 1).start()

    def teacher_out(i):
        other = device_to[i]
        return remote(staged.at[other], teacher.at[me], t_send.at[i], t_recv.at[me], other)

    def teacher_from(other):
        return remote(staged.at[other], teacher.at[other], t_send.at[0], t_recv.at[other], other)

    for i in range(n - 1):
        teacher_out(i).start()

    teacher[me] = staged[me]

    spots = [c for c, _ in tiles(block, 128)]

    def spread(op, values, carry):
        carry = list(carry)
        for i, value in enumerate(values):
            carry[i % 4] = op(carry[i % 4], value)
        return tuple(carry)

    def gather4(op, carry):
        return op(op(carry[0], carry[1]), op(carry[2], carry[3]))

    top = lax.fori_loop(
        0, n,
        lambda j, carry: spread(jnp.maximum, [staged[j, :, c : c + 128].astype(F32) for c in spots], carry),
        (jnp.full((rows, 128), -jnp.inf, F32),) * 4,
    )
    top = jnp.max(gather4(jnp.maximum, top), axis=1, keepdims=True)
    total = lax.fori_loop(
        0, n,
        lambda j, carry: spread(
            jnp.add, [jnp.exp(staged[j, :, c : c + 128].astype(F32) - top) for c in spots], carry
        ),
        (jnp.zeros((rows, 128), F32),) * 4,
    )
    norm_mine = top + jnp.log(jnp.sum(gather4(jnp.add, total), axis=1, keepdims=True))

    for i in range(chips - 1):
        hidden_in(i).wait_recv()
        forward(i).start()

    def unpack(which):
        base = pl.multiple_of(which * half, half)
        flat = gathered[pl.ds(pl.multiple_of(which * chips, chips), chips)].astype(F32).reshape(half, width)
        hid[pl.ds(base, half), :] = flat.astype(BF16)
        hid_t[:, pl.ds(base, half)] = flat.T.astype(BF16)

    unpack(core)

    for i in range(chips):
        forwarded(i).wait_recv()

    unpack(1 - core)
    head_in.wait()

    for start, size in tiles(block, 512):
        diff[:, start : start + size] = jnp.dot(
            hid[...], head[:, start : start + size], preferred_element_type=F32
        )

    group = 64

    @pl.loop(0, tokens // group)
    def _(b):
        at = pl.ds(pl.multiple_of(b * group, group), group)
        top = diff[at, 0:128]
        for c in spots[1:]:
            top = jnp.maximum(top, diff[at, c : c + 128])
        top = jnp.broadcast_to(jnp.max(top, axis=1, keepdims=True), (group, 128))
        peaks[at, :] = top
        total = jnp.zeros((group, 128), F32)
        for c in spots:
            e = jnp.exp(diff[at, c : c + 128] - top)
            expo[at, c : c + 128] = e
            total = total + e
        masses[at, :] = total

    norms[...] = jnp.zeros_like(norms)
    norms[pl.ds(pl.multiple_of(my_block * rows, rows), rows), :] = jnp.broadcast_to(norm_mine, (rows, 128))
    peak = peaks[...].T[0:1, :]
    mass = jnp.sum(masses[...].T, axis=0, keepdims=True)
    lse = peak + jnp.log(mass)
    norm_row = norms[...].T[0:1, :]
    lane = lax.broadcasted_iota(jnp.int32, (rows, 128), 1).astype(F32)

    @pl.loop(0, n)
    def _(step):
        near_y = lax.rem(y + 2 + lax.div(step, 2 * side), side)
        near_x = lax.rem(x + 2 + lax.div(step, 2), side)
        other = (near_y * side + near_x) * 2 + lax.rem(step, 2)

        @pl.when(other != me)
        def _():
            teacher_from(other).wait_recv()

        at = pl.ds(pl.multiple_of((lax.rem(step, 2) * chips + near_y * side + near_x) * rows, rows), rows)
        picked = tok_col[at, :] - lane
        cross = [jnp.zeros((rows, 128), F32)] * 4
        hit = [jnp.zeros((rows, 128), F32)] * 4
        for i, c in enumerate(spots):
            u = diff[at, c : c + 128] - teacher[other, :, c : c + 128].astype(F32)
            diff[at, c : c + 128] = u
            cross[i % 4] = cross[i % 4] + expo[at, c : c + 128] * u
            hit[i % 4] = hit[i % 4] + jnp.where(picked == float(c), u, 0.0)
        crosses[at, :] = gather4(jnp.add, cross)
        hits[at, :] = gather4(jnp.add, hit)

    row = lax.broadcasted_iota(jnp.int32, (4, tokens), 0)

    def rows_of(values):
        out = jnp.zeros((4, tokens), F32)
        for i, value in enumerate(values):
            out = jnp.where(row == i, value, out)
        return out

    own = rows_of([
        lse,
        jnp.sum(crosses[...].T, axis=0, keepdims=True) / mass,
        jnp.sum(hits[...].T, axis=0, keepdims=True),
        norm_row,
    ])
    stat_out[...] = own
    stat_in[me] = own

    def stat_to(i):
        return remote(stat_out, stat_in.at[me], s_send.at[i], s_recv.at[i], device_to[i])

    def stat_from(i):
        return remote(stat_out, stat_in.at[device_from[i]], s_send.at[i], s_recv.at[i], device_to[i])

    for i in range(n - 1):
        stat_to(i).start()
    for i in range(n - 1):
        stat_from(i).wait_recv()

    top = functools.reduce(jnp.maximum, [stat_in[d] for d in range(n)])[0:1, :]
    total = jnp.zeros((4, tokens), F32)
    for d in range(n):
        block_stat = stat_in[d]
        weight = jnp.exp(block_stat[0:1, :] - top)
        total = total + jnp.where(row == 0, weight, jnp.where(row == 1, weight * block_stat, block_stat))
    mass, cross, hit, norm_teacher = (total[i : i + 1, :] for i in range(4))
    norm_student = top + jnp.log(mass)
    mean = cross / mass
    sampled = hit - norm_student + norm_teacher
    div = mean - norm_student + norm_teacher
    scale = jnp.exp(peak - norm_student)
    shift = mean + sampled
    final = rows_of([scale, shift, sampled, div])
    columns = jnp.concatenate([final, jnp.zeros((124, tokens), F32)], axis=0).T
    stat[...] = columns
    halves = columns.reshape(2, chips, rows, 128)
    ordered = jnp.stack([halves[0], halves[1]], axis=1).reshape(tokens, 128)
    div_ref[...] = ordered.T[3:4, :]

    span = 32

    @pl.loop(0, tokens // span)
    def _(b):
        at = pl.ds(pl.multiple_of(b * span, span), span)
        wide = lax.broadcasted_iota(jnp.int32, (span, 128), 1).astype(F32)
        picked = tok_col[at, :] - wide
        scale = jnp.broadcast_to(stat[at, 0:1], (span, 128))
        shift = jnp.broadcast_to(stat[at, 1:2], (span, 128))
        sampled = jnp.broadcast_to(stat[at, 2:3], (span, 128))
        for c in spots:
            g = expo[at, c : c + 128] * (scale * (diff[at, c : c + 128] - shift))
            g = g + jnp.where(picked == float(c), sampled, 0.0)
            grad[at, c : c + 128] = g.astype(BF16)

    own_rows = pl.ds(pl.multiple_of(core * half, half), half)
    sib_rows = pl.ds(pl.multiple_of((1 - core) * half, half), half)
    pieces = tiles(width, 256)

    def pair(i):
        return remote(part_sib.at[i], pair_in.at[i], p_send.at[i], p_recv.at[i], sibling)

    for i, (start, size) in enumerate(pieces):
        part = lax.dot_general(
            grad[...], head[start : start + size, :], (((1,), (1,)), ((), ())), preferred_element_type=F32
        )
        stat_rows = jnp.where(core == 0, part[half:], part[:half])
        part_sib[i] = stat_rows
        part_own[i] = jnp.where(core == 0, part[:half], part[half:])
        pair(i).start()

    for i, (start, size) in enumerate(pieces):
        pair(i).wait_recv()
        total = part_own[i] + pair_in[i]
        part_own[i] = total
        red_out[:, :, start : start + size] = total.reshape(chips, rows, size).astype(BF16)

    def reduce_to(i):
        return remote(red_out.at[chip_to[i]], red_in.at[chip], r_send.at[i], r_recv.at[i], chip_to[i] * 2 + core)

    def reduce_from(i):
        return remote(red_out.at[chip], red_in.at[chip_from[i]], r_send.at[i], r_recv.at[i], chip_to[i] * 2 + core)

    for i in range(chips - 1):
        reduce_to(i).start()

    red_in[chip] = jnp.zeros((rows, width), BF16)

    for start, size in tiles(block, 256):
        wgrad_ref[:, start : start + size] = jnp.dot(
            hid_t[...], grad[:, start : start + size], preferred_element_type=F32
        ).astype(BF16)

    for i in range(chips - 1):
        reduce_from(i).wait_recv()

    at = pl.ds(pl.multiple_of(chip * rows, rows), rows)
    for i, (start, size) in enumerate(pieces):
        total = part_own[i, at, :]
        for k in range(chips):
            total = total + red_in[k, :, start : start + size].astype(F32)
        hgrad_ref[:, start : start + size] = total.astype(BF16)

    for i in range(chips - 1):
        hidden_out(i).wait_send()
        reduce_to(i).wait_send()
    for i in range(chips):
        forward(i).wait_send()
    for i in range(n - 1):
        teacher_out(i).wait_send()
        stat_to(i).wait_send()
    for i in range(len(pieces)):
        pair(i).wait_send()


def out_kernel(div, hgrad, wgrad, div_out, hgrad_out, wgrad_out, sem):
    strip = wgrad.shape[0] // 8
    copies = [
        pltpu.make_async_copy(wgrad.at[pl.ds(i * strip, strip)], wgrad_out.at[pl.ds(i * strip, strip)], sem.at[i])
        for i in range(8)
    ]
    copies.append(pltpu.make_async_copy(div, div_out, sem.at[8]))
    copies.append(pltpu.make_async_copy(hgrad, hgrad_out, sem.at[9]))
    for copy in copies:
        copy.start()
    for copy in copies:
        copy.wait()


def on_device(hidden, head_weight, teacher_logits, token_ids, teacher_map, student_map):
    n = lax.axis_size("voc")
    chips = n // 2
    rows, width = hidden.shape
    block = head_weight.shape[1]
    tokens = n * rows
    half = chips * rows
    pieces = len(tiles(width, 256))
    dma = pltpu.SemaphoreType.DMA
    vmem = pl.BlockSpec(memory_space=pltpu.VMEM)
    hbm = pl.BlockSpec(memory_space=pltpu.HBM)
    div, hgrad, wgrad = pl.pallas_call(
        functools.partial(kernel, n),
        out_shape=(
            pltpu.VMEM((1, tokens), F32),
            pltpu.VMEM((rows, width), BF16),
            pltpu.VMEM((width, block), BF16),
        ),
        in_specs=[hbm] * 6,
        out_specs=(vmem, vmem, vmem),
        scratch_shapes=[
            pltpu.VMEM((1, tokens), jnp.int32),
            pltpu.SMEM((n,), jnp.int32),
            pltpu.SMEM((n,), jnp.int32),
            pltpu.VMEM((width, block), BF16),
            pltpu.VMEM((n, rows, block), BF16),
            pltpu.VMEM((n, rows, block), BF16),
            pltpu.VMEM((n, rows, block), BF16),
            pltpu.VMEM((n, rows, width), BF16),
            pltpu.VMEM((tokens, width), BF16),
            pltpu.VMEM((width, tokens), BF16),
            pltpu.VMEM((tokens, block), BF16),
            pltpu.VMEM((tokens, block), F32),
            pltpu.VMEM((tokens, block), F32),
            pltpu.VMEM((tokens, 128), F32),
            pltpu.VMEM((tokens, 128), F32),
            pltpu.VMEM((tokens, 128), F32),
            pltpu.VMEM((tokens, 128), F32),
            pltpu.VMEM((tokens, 128), F32),
            pltpu.VMEM((tokens, 128), F32),
            pltpu.VMEM((tokens, 128), F32),
            pltpu.VMEM((4, tokens), F32),
            pltpu.VMEM((n, 4, tokens), F32),
            pltpu.VMEM((pieces, half, 256), F32),
            pltpu.VMEM((pieces, half, 256), F32),
            pltpu.VMEM((pieces, half, 256), F32),
            pltpu.VMEM((chips, rows, width), BF16),
            pltpu.VMEM((chips, rows, width), BF16),
            dma((5,)),
            dma((n,)),
            dma((n,)),
            dma((n,)),
            dma((chips,)),
            dma((chips,)),
            dma((chips,)),
            dma((chips,)),
            dma((n,)),
            dma((n,)),
            dma((pieces,)),
            dma((pieces,)),
            dma((chips,)),
            dma((chips,)),
        ],
        compiler_params=pltpu.CompilerParams(
            collective_id=0, has_side_effects=True, vmem_limit_bytes=48 * 1024 * 1024
        ),
    )(*(
        pltpu.with_memory_space_constraint(x, pltpu.HBM)
        for x in (hidden, head_weight, teacher_logits, token_ids.reshape(1, tokens), teacher_map, student_map)
    ))
    div, hgrad, wgrad = pl.pallas_call(
        out_kernel,
        out_shape=(
            jax.ShapeDtypeStruct((1, tokens), F32),
            jax.ShapeDtypeStruct((rows, width), BF16),
            jax.ShapeDtypeStruct((width, block), BF16),
        ),
        in_specs=[vmem] * 3,
        out_specs=(hbm,) * 3,
        scratch_shapes=[dma((10,))],
        compiler_params=pltpu.CompilerParams(vmem_limit_bytes=2 * 1024 * 1024),
    )(*(pltpu.with_memory_space_constraint(x, pltpu.VMEM) for x in (div, hgrad, wgrad)))
    return div.reshape(tokens), hgrad, wgrad


def solution(mesh):
    return jax.shard_map(
        on_device,
        mesh=mesh,
        in_specs=(
            P(("grp", "voc"), None),
            P(None, "voc"),
            P(("grp", "voc"), None),
            P("grp"),
            P(),
            P(),
        ),
        out_specs=(P("grp"), P(("grp", "voc"), None), P(None, ("grp", "voc"))),
        check_vma=False,
    )
```

```python
import functools
import math

import jax
import jax.numpy as jnp
from jax import lax
from jax.experimental import pallas as pl
from jax.experimental.pallas import tpu as pltpu
from jax.sharding import PartitionSpec as P

MESH = pl.DeviceIdType.MESH
F32 = jnp.float32
BF16 = jnp.bfloat16


def tiles(width, size):
    return [(start, min(size, width - start)) for start in range(0, width, size)]


def kernel(
    n,
    hidden_ref,
    head_ref,
    teacher_ref,
    token_hbm,
    teacher_map_hbm,
    student_map_hbm,
    div_ref,
    hgrad_ref,
    wgrad_ref,
    token_ref,
    teacher_map,
    student_map,
    head,
    mine,
    staged,
    teacher,
    gathered,
    hid,
    hid_t,
    grad,
    head_t,
    diff,
    expo,
    tok_col,
    stat,
    peaks,
    masses,
    norms,
    crosses,
    hits,
    stat_out,
    stat_in,
    parts,
    pair_in,
    red_out,
    red_in,
    local_sem,
    m_sem,
    t_send,
    t_recv,
    h_send,
    h_recv,
    f_send,
    f_recv,
    s_send,
    s_recv,
    p_send,
    p_recv,
    r_send,
    r_recv,
):
    chips = n // 2
    rows, width = hidden_ref.shape
    block = head_ref.shape[1]
    half = chips * rows
    tokens = 2 * half
    side = math.isqrt(chips)
    me = lax.axis_index("voc")
    core, chip = lax.rem(me, 2), lax.div(me, 2)
    y, x = lax.div(chip, side), lax.rem(chip, side)
    sibling = me + 1 - 2 * core
    my_block = core * chips + chip

    ys = [lax.rem(y + d, side) * side for d in range(side)]
    xs = [lax.rem(x + d, side) for d in range(side)]

    def far(d):
        return -sum(min(v, side - v) for v in d[:2])

    def back(d):
        return (-d[0] % side, -d[1] % side) + d[2:]

    chip_deltas = sorted([(dy, dx) for dy in range(side) for dx in range(side) if dy or dx], key=far)
    device_deltas = sorted([d + (c,) for d in chip_deltas + [(0, 0)] for c in (0, 1)][:-2], key=far) + [(0, 0, 1)]
    cores = [core, 1 - core]

    def chip_at(d):
        return ys[d[0]] + xs[d[1]]

    def device_at(d):
        return chip_at(d) * 2 + cores[d[2]]

    chip_to = [chip_at(d) for d in chip_deltas]
    chip_from = [chip_at(back(d)) for d in chip_deltas]
    device_to = [device_at(d) for d in device_deltas]
    device_from = [device_at(back(d)) for d in device_deltas]

    def remote(src, dst, send, recv, device):
        return pltpu.make_async_remote_copy(
            src_ref=src, dst_ref=dst, send_sem=send, recv_sem=recv,
            device_id={"voc": device}, device_id_type=MESH,
        )

    barrier = pltpu.get_barrier_semaphore()

    for other in device_to:
        pl.semaphore_signal(barrier, inc=1, device_id={"voc": other}, device_id_type=MESH)

    small = [
        pltpu.make_async_copy(token_hbm, token_ref, local_sem.at[1]),
        pltpu.make_async_copy(teacher_map_hbm, teacher_map, local_sem.at[2]),
        pltpu.make_async_copy(student_map_hbm, student_map, local_sem.at[3]),
        pltpu.make_async_copy(hidden_ref, gathered.at[my_block], local_sem.at[4]),
    ]
    for copy in small:
        copy.start()

    def teacher_in(p):
        return pltpu.make_async_copy(
            teacher_ref.at[:, pl.ds(pl.multiple_of(p * block, 128), block)], mine.at[p], m_sem.at[p]
        )

    @pl.loop(0, n)
    def _(p):
        teacher_in(p).start()

    head_in = pltpu.make_async_copy(head_ref, head, local_sem.at[0])
    head_in.start()

    for copy in small:
        copy.wait()

    eye = (
        lax.broadcasted_iota(jnp.int32, (tokens, tokens), 0)
        == lax.broadcasted_iota(jnp.int32, (tokens, tokens), 1)
    )
    ids = jnp.sum(jnp.where(eye, token_ref[...].astype(F32), 0.0), axis=1, keepdims=True)
    ids = ids - (student_map[me] * block).astype(F32)
    ids = jnp.broadcast_to(ids, (tokens, 128)).reshape(chips, 2, rows, 128)
    tok_col[...] = jnp.concatenate([ids[:, 0], ids[:, 1]], axis=0).reshape(tokens, 128)

    place = lax.broadcasted_iota(jnp.int32, (1, tokens), 1) // rows
    teacher_id = jnp.zeros((1, tokens), F32)
    student_id = jnp.zeros((1, tokens), F32)
    for p in range(n):
        teacher_id = jnp.where(place == p, teacher_map[p].astype(F32), teacher_id)
        student_id = jnp.where(place == p, student_map[p].astype(F32), student_id)
    wanted = jnp.sum(jnp.where(eye, student_id, 0.0), axis=1, keepdims=True)
    same_row = (
        lax.broadcasted_iota(jnp.int32, (tokens, tokens), 0) % rows
        == lax.broadcasted_iota(jnp.int32, (tokens, tokens), 1) % rows
    )
    move = jnp.where(jnp.logical_and(wanted == teacher_id, same_row), 1.0, 0.0).astype(BF16)

    @pl.loop(0, n)
    def _(p):
        teacher_in(p).wait()

    for start, size in tiles(block, 256):
        piece = mine[:, :, start : start + size].astype(F32).reshape(tokens, size).astype(BF16)
        piece = jnp.dot(move, piece, preferred_element_type=F32)
        staged[:, :, start : start + size] = piece.reshape(n, rows, size).astype(BF16)

    pl.semaphore_wait(barrier, n - 1)

    def hidden_out(i):
        return remote(
            gathered.at[my_block], gathered.at[my_block], h_send.at[i], h_recv.at[i], chip_to[i] * 2 + core
        )

    def hidden_in(i):
        landed = gathered.at[core * chips + chip_from[i]]
        return remote(landed, landed, h_send.at[i], h_recv.at[i], chip_to[i] * 2 + core)

    def forward(i):
        landed = gathered.at[my_block if i == chips - 1 else core * chips + chip_from[i]]
        return remote(landed, landed, f_send.at[i], f_recv.at[i], sibling)

    def forwarded(i):
        landed = gathered.at[(1 - core) * chips + (chip if i == chips - 1 else chip_from[i])]
        return remote(landed, landed, f_send.at[i], f_recv.at[i], sibling)

    for i in range(chips - 1):
        hidden_out(i).start()
    forward(chips - 1).start()

    def teacher_out(i):
        other = device_to[i]
        return remote(staged.at[other], teacher.at[me], t_send.at[i], t_recv.at[me], other)

    def teacher_from(other):
        return remote(staged.at[other], teacher.at[other], t_send.at[0], t_recv.at[other], other)

    for i in range(10):
        teacher_out(i).start()

    teacher[me] = staged[me]

    spots = [c for c, _ in tiles(block, 128)]

    def spread(op, values, carry):
        carry = list(carry)
        for i, value in enumerate(values):
            carry[i % 4] = op(carry[i % 4], value)
        return tuple(carry)

    def gather4(op, carry):
        return op(op(carry[0], carry[1]), op(carry[2], carry[3]))

    top = lax.fori_loop(
        0, n,
        lambda j, carry: spread(jnp.maximum, [staged[j, :, c : c + 128].astype(F32) for c in spots], carry),
        (jnp.full((rows, 128), -jnp.inf, F32),) * 4,
    )
    top = jnp.max(gather4(jnp.maximum, top), axis=1, keepdims=True)
    total = lax.fori_loop(
        0, n,
        lambda j, carry: spread(
            jnp.add, [jnp.exp(staged[j, :, c : c + 128].astype(F32) - top) for c in spots], carry
        ),
        (jnp.zeros((rows, 128), F32),) * 4,
    )
    norm_mine = top + jnp.log(jnp.sum(gather4(jnp.add, total), axis=1, keepdims=True))

    head_in.wait()

    @pl.loop(0, block // 128)
    def _(b):
        at = pl.ds(pl.multiple_of(b * 128, 128), 128)
        head_t[at, :] = head[:, at].T

    for i in range(10, n - 1):
        teacher_out(i).start()

    for i in range(chips - 1):
        hidden_in(i).wait_recv()
        forward(i).start()

    def unpack(which):
        base = pl.multiple_of(which * half, half)
        flat = gathered[pl.ds(pl.multiple_of(which * chips, chips), chips)].astype(F32).reshape(half, width)
        hid[pl.ds(base, half), :] = flat.astype(BF16)
        hid_t[:, pl.ds(base, half)] = flat.T.astype(BF16)

    unpack(core)

    for i in range(chips):
        forwarded(i).wait_recv()

    unpack(1 - core)

    for start, size in tiles(block, 512):
        diff[:, start : start + size] = jnp.dot(
            hid[...], head[:, start : start + size], preferred_element_type=F32
        )

    group = 64

    @pl.loop(0, tokens // group)
    def _(b):
        at = pl.ds(pl.multiple_of(b * group, group), group)
        top = diff[at, 0:128]
        for c in spots[1:]:
            top = jnp.maximum(top, diff[at, c : c + 128])
        top = jnp.broadcast_to(jnp.max(top, axis=1, keepdims=True), (group, 128))
        peaks[at, :] = top
        total = jnp.zeros((group, 128), F32)
        for c in spots:
            e = jnp.exp(diff[at, c : c + 128] - top)
            expo[at, c : c + 128] = e
            total = total + e
        masses[at, :] = total

    norms[...] = jnp.zeros_like(norms)
    norms[pl.ds(pl.multiple_of(my_block * rows, rows), rows), :] = jnp.broadcast_to(norm_mine, (rows, 128))
    peak = peaks[...].T[0:1, :]
    mass = jnp.sum(masses[...].T, axis=0, keepdims=True)
    lse = peak + jnp.log(mass)
    norm_row = norms[...].T[0:1, :]
    lane = lax.broadcasted_iota(jnp.int32, (rows, 128), 1).astype(F32)

    @pl.loop(0, n)
    def _(step):
        near_y = lax.rem(y + 2 + lax.div(step, 2 * side), side)
        near_x = lax.rem(x + 2 + lax.div(step, 2), side)
        other = (near_y * side + near_x) * 2 + lax.rem(step, 2)

        @pl.when(other != me)
        def _():
            teacher_from(other).wait_recv()

        at = pl.ds(pl.multiple_of((lax.rem(step, 2) * chips + near_y * side + near_x) * rows, rows), rows)
        picked = tok_col[at, :] - lane
        cross = [jnp.zeros((rows, 128), F32)] * 4
        hit = [jnp.zeros((rows, 128), F32)] * 4
        for i, c in enumerate(spots):
            u = diff[at, c : c + 128] - teacher[other, :, c : c + 128].astype(F32)
            diff[at, c : c + 128] = u
            cross[i % 4] = cross[i % 4] + expo[at, c : c + 128] * u
            hit[i % 4] = hit[i % 4] + jnp.where(picked == float(c), u, 0.0)
        crosses[at, :] = gather4(jnp.add, cross)
        hits[at, :] = gather4(jnp.add, hit)

    row = lax.broadcasted_iota(jnp.int32, (4, tokens), 0)

    def rows_of(values):
        out = jnp.zeros((4, tokens), F32)
        for i, value in enumerate(values):
            out = jnp.where(row == i, value, out)
        return out

    own = rows_of([
        lse,
        jnp.sum(crosses[...].T, axis=0, keepdims=True) / mass,
        jnp.sum(hits[...].T, axis=0, keepdims=True),
        norm_row,
    ])
    stat_out[...] = own
    stat_in[me] = own

    def stat_to(i):
        return remote(stat_out, stat_in.at[me], s_send.at[i], s_recv.at[i], device_to[i])

    def stat_from(i):
        return remote(stat_out, stat_in.at[device_from[i]], s_send.at[i], s_recv.at[i], device_to[i])

    for i in range(n - 1):
        stat_to(i).start()
    for i in range(n - 1):
        stat_from(i).wait_recv()

    top = functools.reduce(jnp.maximum, [stat_in[d] for d in range(n)])[0:1, :]
    total = jnp.zeros((4, tokens), F32)
    for d in range(n):
        block_stat = stat_in[d]
        weight = jnp.exp(block_stat[0:1, :] - top)
        total = total + jnp.where(row == 0, weight, jnp.where(row == 1, weight * block_stat, block_stat))
    mass, cross, hit, norm_teacher = (total[i : i + 1, :] for i in range(4))
    norm_student = top + jnp.log(mass)
    mean = cross / mass
    sampled = hit - norm_student + norm_teacher
    div = mean - norm_student + norm_teacher
    scale = jnp.exp(peak - norm_student)
    shift = mean + sampled
    final = rows_of([scale, shift, sampled, div])
    columns = jnp.concatenate([final, jnp.zeros((124, tokens), F32)], axis=0).T
    stat[...] = columns
    span = 32

    @pl.loop(0, tokens // span)
    def _(b):
        at = pl.ds(pl.multiple_of(b * span, span), span)
        wide = lax.broadcasted_iota(jnp.int32, (span, 128), 1).astype(F32)
        picked = tok_col[at, :] - wide
        scale = jnp.broadcast_to(stat[at, 0:1], (span, 128))
        shift = jnp.broadcast_to(stat[at, 1:2], (span, 128))
        sampled = jnp.broadcast_to(stat[at, 2:3], (span, 128))
        for c in spots:
            g = expo[at, c : c + 128] * (scale * (diff[at, c : c + 128] - shift))
            g = g + jnp.where(picked == float(c), sampled, 0.0)
            grad[at, c : c + 128] = g.astype(BF16)

    own_rows = pl.ds(pl.multiple_of(core * half, half), half)
    sib_rows = pl.ds(pl.multiple_of((1 - core) * half, half), half)
    pieces = tiles(width, 256)

    def pair(i):
        return remote(parts.at[i, sib_rows], pair_in.at[i], p_send.at[i], p_recv.at[i], sibling)

    cuts = [(0, 3), (3, len(pieces))]

    def span_of(k):
        first, last = cuts[k]
        return slice(pieces[first][0], pieces[last - 1][0] + pieces[last - 1][1])

    def reduce_to(i, k):
        return remote(
            red_out.at[chip_to[i], :, span_of(k)], red_in.at[chip, :, span_of(k)],
            r_send.at[k, i], r_recv.at[k, i], chip_to[i] * 2 + core,
        )

    def reduce_from(i, k):
        return remote(
            red_out.at[chip, :, span_of(k)], red_in.at[chip_from[i], :, span_of(k)],
            r_send.at[k, i], r_recv.at[k, i], chip_to[i] * 2 + core,
        )

    def multiply(k):
        for i in range(*cuts[k]):
            start, size = pieces[i]
            parts[i] = jnp.dot(grad[...], head_t[:, start : start + size], preferred_element_type=F32)
            pair(i).start()

    def spread_sums(k):
        for i in range(*cuts[k]):
            start, size = pieces[i]
            pair(i).wait_recv()
            total = parts[i, own_rows] + pair_in[i]
            parts[i, own_rows] = total
            red_out[:, :, start : start + size] = total.reshape(chips, rows, size).astype(BF16)
        for i in range(chips - 1):
            reduce_to(i, k).start()

    multiply(0)
    multiply(1)
    spread_sums(0)
    spread_sums(1)

    halves = stat[...].reshape(2, chips, rows, 128)
    ordered = jnp.stack([halves[0], halves[1]], axis=1).reshape(tokens, 128)
    div_ref[...] = ordered.T[3:4, :]
    red_in[chip] = jnp.zeros((rows, width), BF16)

    for start, size in tiles(block, 256):
        wgrad_ref[:, start : start + size] = jnp.dot(
            hid_t[...], grad[:, start : start + size], preferred_element_type=F32
        ).astype(BF16)

    for i in range(chips - 1):
        reduce_from(i, 0).wait_recv()
        reduce_from(i, 1).wait_recv()

    at = pl.ds(pl.multiple_of(my_block * rows, rows), rows)
    for i, (start, size) in enumerate(pieces):
        total = parts[i, at, :]
        for k in range(chips):
            total = total + red_in[k, :, start : start + size].astype(F32)
        hgrad_ref[:, start : start + size] = total.astype(BF16)

    for i in range(chips - 1):
        hidden_out(i).wait_send()
        reduce_to(i, 0).wait_send()
        reduce_to(i, 1).wait_send()
    for i in range(chips):
        forward(i).wait_send()
    for i in range(n - 1):
        teacher_out(i).wait_send()
        stat_to(i).wait_send()
    for i in range(len(pieces)):
        pair(i).wait_send()


def out_kernel(div, hgrad, wgrad, div_out, hgrad_out, wgrad_out, sem):
    strip = wgrad.shape[0] // 8
    copies = [
        pltpu.make_async_copy(wgrad.at[pl.ds(i * strip, strip)], wgrad_out.at[pl.ds(i * strip, strip)], sem.at[i])
        for i in range(8)
    ]
    copies.append(pltpu.make_async_copy(div, div_out, sem.at[8]))
    copies.append(pltpu.make_async_copy(hgrad, hgrad_out, sem.at[9]))
    for copy in copies:
        copy.start()
    for copy in copies:
        copy.wait()


def on_device(hidden, head_weight, teacher_logits, token_ids, teacher_map, student_map):
    n = lax.axis_size("voc")
    chips = n // 2
    rows, width = hidden.shape
    block = head_weight.shape[1]
    tokens = n * rows
    half = chips * rows
    pieces = len(tiles(width, 256))
    dma = pltpu.SemaphoreType.DMA
    vmem = pl.BlockSpec(memory_space=pltpu.VMEM)
    hbm = pl.BlockSpec(memory_space=pltpu.HBM)
    div, hgrad, wgrad = pl.pallas_call(
        functools.partial(kernel, n),
        out_shape=(
            pltpu.VMEM((1, tokens), F32),
            pltpu.VMEM((rows, width), BF16),
            pltpu.VMEM((width, block), BF16),
        ),
        in_specs=[hbm] * 6,
        out_specs=(vmem, vmem, vmem),
        scratch_shapes=[
            pltpu.VMEM((1, tokens), jnp.int32),
            pltpu.SMEM((n,), jnp.int32),
            pltpu.SMEM((n,), jnp.int32),
            pltpu.VMEM((width, block), BF16),
            pltpu.VMEM((n, rows, block), BF16),
            pltpu.VMEM((n, rows, block), BF16),
            pltpu.VMEM((n, rows, block), BF16),
            pltpu.VMEM((n, rows, width), BF16),
            pltpu.VMEM((tokens, width), BF16),
            pltpu.VMEM((width, tokens), BF16),
            pltpu.VMEM((tokens, block), BF16),
            pltpu.VMEM((block, width), BF16),
            pltpu.VMEM((tokens, block), F32),
            pltpu.VMEM((tokens, block), F32),
            pltpu.VMEM((tokens, 128), F32),
            pltpu.VMEM((tokens, 128), F32),
            pltpu.VMEM((tokens, 128), F32),
            pltpu.VMEM((tokens, 128), F32),
            pltpu.VMEM((tokens, 128), F32),
            pltpu.VMEM((tokens, 128), F32),
            pltpu.VMEM((tokens, 128), F32),
            pltpu.VMEM((4, tokens), F32),
            pltpu.VMEM((n, 4, tokens), F32),
            pltpu.VMEM((pieces, tokens, 256), F32),
            pltpu.VMEM((pieces, half, 256), F32),
            pltpu.VMEM((chips, rows, width), BF16),
            pltpu.VMEM((chips, rows, width), BF16),
            dma((5,)),
            dma((n,)),
            dma((n,)),
            dma((n,)),
            dma((chips,)),
            dma((chips,)),
            dma((chips,)),
            dma((chips,)),
            dma((n,)),
            dma((n,)),
            dma((pieces,)),
            dma((pieces,)),
            dma((2, chips)),
            dma((2, chips)),
        ],
        compiler_params=pltpu.CompilerParams(
            collective_id=0, has_side_effects=True, vmem_limit_bytes=48 * 1024 * 1024
        ),
    )(*(
        pltpu.with_memory_space_constraint(x, pltpu.HBM)
        for x in (hidden, head_weight, teacher_logits, token_ids.reshape(1, tokens), teacher_map, student_map)
    ))
    div, hgrad, wgrad = pl.pallas_call(
        out_kernel,
        out_shape=(
            jax.ShapeDtypeStruct((1, tokens), F32),
            jax.ShapeDtypeStruct((rows, width), BF16),
            jax.ShapeDtypeStruct((width, block), BF16),
        ),
        in_specs=[vmem] * 3,
        out_specs=(hbm,) * 3,
        scratch_shapes=[dma((10,))],
        compiler_params=pltpu.CompilerParams(vmem_limit_bytes=2 * 1024 * 1024),
    )(*(pltpu.with_memory_space_constraint(x, pltpu.VMEM) for x in (div, hgrad, wgrad)))
    return div.reshape(tokens), hgrad, wgrad


def solution(mesh):
    return jax.shard_map(
        on_device,
        mesh=mesh,
        in_specs=(
            P(("grp", "voc"), None),
            P(None, "voc"),
            P(("grp", "voc"), None),
            P("grp"),
            P(),
            P(),
        ),
        out_specs=(P("grp"), P(("grp", "voc"), None), P(None, ("grp", "voc"))),
        check_vma=False,
    )
```

```python
import functools
import math

import jax
import jax.numpy as jnp
from jax import lax
from jax.experimental import pallas as pl
from jax.experimental.pallas import tpu as pltpu
from jax.sharding import PartitionSpec as P

MESH = pl.DeviceIdType.MESH
F32 = jnp.float32
BF16 = jnp.bfloat16


def tiles(width, size):
    return [(start, min(size, width - start)) for start in range(0, width, size)]


def kernel(
    n,
    hidden_ref,
    head_ref,
    teacher_ref,
    token_hbm,
    teacher_map_hbm,
    student_map_hbm,
    div_ref,
    hgrad_ref,
    wgrad_ref,
    token_ref,
    teacher_map,
    student_map,
    head,
    mine,
    staged,
    teacher,
    gathered,
    hid,
    hid_t,
    grad,
    head_t,
    diff,
    expo,
    tok_col,
    stat,
    peaks,
    masses,
    norms,
    crosses,
    hits,
    stat_out,
    stat_in,
    parts,
    pair_in,
    red_out,
    red_in,
    local_sem,
    m_sem,
    t_send,
    t_recv,
    h_send,
    h_recv,
    f_send,
    f_recv,
    s_send,
    s_recv,
    p_send,
    p_recv,
    r_send,
    r_recv,
):
    chips = n // 2
    rows, width = hidden_ref.shape
    block = head_ref.shape[1]
    half = chips * rows
    tokens = 2 * half
    side = math.isqrt(chips)
    me = lax.axis_index("voc")
    core, chip = lax.rem(me, 2), lax.div(me, 2)
    y, x = lax.div(chip, side), lax.rem(chip, side)
    sibling = me + 1 - 2 * core
    my_block = core * chips + chip

    ys = [lax.rem(y + d, side) * side for d in range(side)]
    xs = [lax.rem(x + d, side) for d in range(side)]

    def far(d):
        return -sum(min(v, side - v) for v in d[:2])

    def back(d):
        return (-d[0] % side, -d[1] % side) + d[2:]

    chip_deltas = sorted([(dy, dx) for dy in range(side) for dx in range(side) if dy or dx], key=far)
    device_deltas = sorted([d + (c,) for d in chip_deltas + [(0, 0)] for c in (0, 1)][:-2], key=far) + [(0, 0, 1)]
    cores = [core, 1 - core]

    def chip_at(d):
        return ys[d[0]] + xs[d[1]]

    def device_at(d):
        return chip_at(d) * 2 + cores[d[2]]

    chip_to = [chip_at(d) for d in chip_deltas]
    chip_from = [chip_at(back(d)) for d in chip_deltas]
    device_to = [device_at(d) for d in device_deltas]
    device_from = [device_at(back(d)) for d in device_deltas]

    def remote(src, dst, send, recv, device):
        return pltpu.make_async_remote_copy(
            src_ref=src, dst_ref=dst, send_sem=send, recv_sem=recv,
            device_id={"voc": device}, device_id_type=MESH,
        )

    barrier = pltpu.get_barrier_semaphore()

    for other in device_to:
        pl.semaphore_signal(barrier, inc=1, device_id={"voc": other}, device_id_type=MESH)

    small = [
        pltpu.make_async_copy(token_hbm, token_ref, local_sem.at[1]),
        pltpu.make_async_copy(teacher_map_hbm, teacher_map, local_sem.at[2]),
        pltpu.make_async_copy(student_map_hbm, student_map, local_sem.at[3]),
        pltpu.make_async_copy(hidden_ref, gathered.at[my_block], local_sem.at[4]),
    ]
    for copy in small:
        copy.start()

    def teacher_in(p):
        return pltpu.make_async_copy(
            teacher_ref.at[:, pl.ds(pl.multiple_of(p * block, 128), block)], mine.at[p], m_sem.at[p]
        )

    @pl.loop(0, n)
    def _(p):
        teacher_in(p).start()

    head_in = pltpu.make_async_copy(head_ref, head, local_sem.at[0])
    head_in.start()

    for copy in small:
        copy.wait()

    eye = (
        lax.broadcasted_iota(jnp.int32, (tokens, tokens), 0)
        == lax.broadcasted_iota(jnp.int32, (tokens, tokens), 1)
    )
    ids = jnp.sum(jnp.where(eye, token_ref[...].astype(F32), 0.0), axis=1, keepdims=True)
    ids = ids - (student_map[me] * block).astype(F32)
    ids = jnp.broadcast_to(ids, (tokens, 128)).reshape(chips, 2, rows, 128)
    tok_col[...] = jnp.concatenate([ids[:, 0], ids[:, 1]], axis=0).reshape(tokens, 128)

    place = lax.broadcasted_iota(jnp.int32, (1, tokens), 1) // rows
    teacher_id = jnp.zeros((1, tokens), F32)
    student_id = jnp.zeros((1, tokens), F32)
    for p in range(n):
        teacher_id = jnp.where(place == p, teacher_map[p].astype(F32), teacher_id)
        student_id = jnp.where(place == p, student_map[p].astype(F32), student_id)
    wanted = jnp.sum(jnp.where(eye, student_id, 0.0), axis=1, keepdims=True)
    same_row = (
        lax.broadcasted_iota(jnp.int32, (tokens, tokens), 0) % rows
        == lax.broadcasted_iota(jnp.int32, (tokens, tokens), 1) % rows
    )
    move = jnp.where(jnp.logical_and(wanted == teacher_id, same_row), 1.0, 0.0).astype(BF16)

    @pl.loop(0, n)
    def _(p):
        teacher_in(p).wait()

    for start, size in tiles(block, 256):
        piece = mine[:, :, start : start + size].astype(F32).reshape(tokens, size).astype(BF16)
        piece = jnp.dot(move, piece, preferred_element_type=F32)
        staged[:, :, start : start + size] = piece.reshape(n, rows, size).astype(BF16)

    pl.semaphore_wait(barrier, n - 1)

    def hidden_out(i):
        return remote(
            gathered.at[my_block], gathered.at[my_block], h_send.at[i], h_recv.at[i], chip_to[i] * 2 + core
        )

    def hidden_in(i):
        landed = gathered.at[core * chips + chip_from[i]]
        return remote(landed, landed, h_send.at[i], h_recv.at[i], chip_to[i] * 2 + core)

    def forward(i):
        landed = gathered.at[my_block if i == chips - 1 else core * chips + chip_from[i]]
        return remote(landed, landed, f_send.at[i], f_recv.at[i], sibling)

    def forwarded(i):
        landed = gathered.at[(1 - core) * chips + (chip if i == chips - 1 else chip_from[i])]
        return remote(landed, landed, f_send.at[i], f_recv.at[i], sibling)

    for i in range(chips - 1):
        hidden_out(i).start()
    forward(chips - 1).start()

    def teacher_out(i):
        other = device_to[i]
        return remote(staged.at[other], teacher.at[me], t_send.at[i], t_recv.at[me], other)

    def teacher_from(other):
        return remote(staged.at[other], teacher.at[other], t_send.at[0], t_recv.at[other], other)

    for i in range(10):
        teacher_out(i).start()

    teacher[me] = staged[me]

    spots = [c for c, _ in tiles(block, 128)]

    def spread(op, values, carry):
        carry = list(carry)
        for i, value in enumerate(values):
            carry[i % 4] = op(carry[i % 4], value)
        return tuple(carry)

    def gather4(op, carry):
        return op(op(carry[0], carry[1]), op(carry[2], carry[3]))

    top = lax.fori_loop(
        0, n,
        lambda j, carry: spread(jnp.maximum, [staged[j, :, c : c + 128].astype(F32) for c in spots], carry),
        (jnp.full((rows, 128), -jnp.inf, F32),) * 4,
    )
    top = jnp.max(gather4(jnp.maximum, top), axis=1, keepdims=True)
    total = lax.fori_loop(
        0, n,
        lambda j, carry: spread(
            jnp.add, [jnp.exp(staged[j, :, c : c + 128].astype(F32) - top) for c in spots], carry
        ),
        (jnp.zeros((rows, 128), F32),) * 4,
    )
    norm_mine = top + jnp.log(jnp.sum(gather4(jnp.add, total), axis=1, keepdims=True))

    head_in.wait()

    @pl.loop(0, block // 128)
    def _(b):
        at = pl.ds(pl.multiple_of(b * 128, 128), 128)
        head_t[at, :] = head[:, at].T

    for i in range(10, n - 1):
        teacher_out(i).start()

    for i in range(chips - 1):
        hidden_in(i).wait_recv()
        forward(i).start()

    def unpack(which):
        base = pl.multiple_of(which * half, half)
        flat = gathered[pl.ds(pl.multiple_of(which * chips, chips), chips)].astype(F32).reshape(half, width)
        hid[pl.ds(base, half), :] = flat.astype(BF16)
        hid_t[:, pl.ds(base, half)] = flat.T.astype(BF16)

    unpack(core)

    for i in range(chips):
        forwarded(i).wait_recv()

    unpack(1 - core)

    for start, size in tiles(block, 512):
        logits = jnp.dot(hid[...], head[:, start : start + size], preferred_element_type=F32)
        diff[:, start : start + size] = logits
        top = functools.reduce(jnp.maximum, [logits[:, c : c + 128] for c in range(0, size, 128)])
        peaks[...] = top if start == 0 else jnp.maximum(peaks[...], top)

    group = 64

    @pl.loop(0, tokens // group)
    def _(b):
        at = pl.ds(pl.multiple_of(b * group, group), group)
        top = peaks[at, :]
        top = jnp.broadcast_to(jnp.max(top, axis=1, keepdims=True), (group, 128))
        peaks[at, :] = top
        total = jnp.zeros((group, 128), F32)
        for c in spots:
            e = jnp.exp(diff[at, c : c + 128] - top)
            expo[at, c : c + 128] = e
            total = total + e
        masses[at, :] = total

    norms[...] = jnp.zeros_like(norms)
    norms[pl.ds(pl.multiple_of(my_block * rows, rows), rows), :] = jnp.broadcast_to(norm_mine, (rows, 128))
    peak = peaks[...].T[0:1, :]
    mass = jnp.sum(masses[...].T, axis=0, keepdims=True)
    lse = peak + jnp.log(mass)
    norm_row = norms[...].T[0:1, :]
    lane = lax.broadcasted_iota(jnp.int32, (rows, 128), 1).astype(F32)

    @pl.loop(0, chips)
    def _(step):
        near_y = lax.rem(y + 2 + lax.div(step, side), side)
        near_x = lax.rem(x + 2 + step, side)
        place = near_y * side + near_x
        for c in range(2):
            other = place * 2 + c

            @pl.when(other != me)
            def _():
                teacher_from(other).wait_recv()

        for c in range(2):
            other = place * 2 + c
            at = pl.ds(pl.multiple_of((c * chips + place) * rows, rows), rows)
            picked = tok_col[at, :] - lane
            cross = [jnp.zeros((rows, 128), F32)] * 2
            hit = [jnp.zeros((rows, 128), F32)] * 2
            for i, spot in enumerate(spots):
                cols = slice(spot, spot + 128)
                u = diff[at, cols] - teacher[other, :, cols].astype(F32)
                diff[at, cols] = u
                cross[i % 2] = cross[i % 2] + expo[at, cols] * u
                hit[i % 2] = hit[i % 2] + jnp.where(picked == float(spot), u, 0.0)
            crosses[at, :] = cross[0] + cross[1]
            hits[at, :] = hit[0] + hit[1]

    row = lax.broadcasted_iota(jnp.int32, (4, tokens), 0)

    def rows_of(values):
        out = jnp.zeros((4, tokens), F32)
        for i, value in enumerate(values):
            out = jnp.where(row == i, value, out)
        return out

    own = rows_of([
        lse,
        jnp.sum(crosses[...].T, axis=0, keepdims=True) / mass,
        jnp.sum(hits[...].T, axis=0, keepdims=True),
        norm_row,
    ])
    stat_out[...] = own
    stat_in[me] = own

    def stat_to(i):
        return remote(stat_out, stat_in.at[me], s_send.at[i], s_recv.at[i], device_to[i])

    def stat_from(i):
        return remote(stat_out, stat_in.at[device_from[i]], s_send.at[i], s_recv.at[i], device_to[i])

    for i in range(n - 1):
        stat_to(i).start()
    for i in range(n - 1):
        stat_from(i).wait_recv()

    top = functools.reduce(jnp.maximum, [stat_in[d] for d in range(n)])[0:1, :]
    total = jnp.zeros((4, tokens), F32)
    for d in range(n):
        block_stat = stat_in[d]
        weight = jnp.exp(block_stat[0:1, :] - top)
        total = total + jnp.where(row == 0, weight, jnp.where(row == 1, weight * block_stat, block_stat))
    mass, cross, hit, norm_teacher = (total[i : i + 1, :] for i in range(4))
    norm_student = top + jnp.log(mass)
    mean = cross / mass
    sampled = hit - norm_student + norm_teacher
    div = mean - norm_student + norm_teacher
    scale = jnp.exp(peak - norm_student)
    shift = mean + sampled
    final = rows_of([scale, shift, sampled, div])
    columns = jnp.concatenate([final, jnp.zeros((124, tokens), F32)], axis=0).T
    stat[...] = columns
    span = 32

    @pl.loop(0, tokens // span)
    def _(b):
        at = pl.ds(pl.multiple_of(b * span, span), span)
        wide = lax.broadcasted_iota(jnp.int32, (span, 128), 1).astype(F32)
        picked = tok_col[at, :] - wide
        scale = jnp.broadcast_to(stat[at, 0:1], (span, 128))
        shift = jnp.broadcast_to(stat[at, 1:2], (span, 128))
        sampled = jnp.broadcast_to(stat[at, 2:3], (span, 128))
        for c in spots:
            g = expo[at, c : c + 128] * (scale * (diff[at, c : c + 128] - shift))
            g = g + jnp.where(picked == float(c), sampled, 0.0)
            grad[at, c : c + 128] = g.astype(BF16)

    own_rows = pl.ds(pl.multiple_of(core * half, half), half)
    sib_rows = pl.ds(pl.multiple_of((1 - core) * half, half), half)
    pieces = tiles(width, 256)

    def pair(i):
        return remote(parts.at[i, sib_rows], pair_in.at[i], p_send.at[i], p_recv.at[i], sibling)

    cuts = [(0, 3), (3, len(pieces))]

    def span_of(k):
        first, last = cuts[k]
        return slice(pieces[first][0], pieces[last - 1][0] + pieces[last - 1][1])

    def reduce_to(i, k):
        return remote(
            red_out.at[chip_to[i], :, span_of(k)], red_in.at[chip, :, span_of(k)],
            r_send.at[k, i], r_recv.at[k, i], chip_to[i] * 2 + core,
        )

    def reduce_from(i, k):
        return remote(
            red_out.at[chip, :, span_of(k)], red_in.at[chip_from[i], :, span_of(k)],
            r_send.at[k, i], r_recv.at[k, i], chip_to[i] * 2 + core,
        )

    def multiply(k):
        for i in range(*cuts[k]):
            start, size = pieces[i]
            parts[i] = jnp.dot(grad[...], head_t[:, start : start + size], preferred_element_type=F32)
            pair(i).start()

    def spread_sums(k):
        for i in range(*cuts[k]):
            start, size = pieces[i]
            pair(i).wait_recv()
            total = parts[i, own_rows] + pair_in[i]
            parts[i, own_rows] = total
            red_out[:, :, start : start + size] = total.reshape(chips, rows, size).astype(BF16)
        for i in range(chips - 1):
            reduce_to(i, k).start()

    multiply(0)
    multiply(1)
    spread_sums(0)
    spread_sums(1)

    halves = stat[...].reshape(2, chips, rows, 128)
    ordered = jnp.stack([halves[0], halves[1]], axis=1).reshape(tokens, 128)
    div_ref[...] = ordered.T[3:4, :]
    red_in[chip] = jnp.zeros((rows, width), BF16)

    for start, size in tiles(block, 256):
        wgrad_ref[:, start : start + size] = jnp.dot(
            hid_t[...], grad[:, start : start + size], preferred_element_type=F32
        ).astype(BF16)

    for i in range(chips - 1):
        reduce_from(i, 0).wait_recv()
        reduce_from(i, 1).wait_recv()

    at = pl.ds(pl.multiple_of(my_block * rows, rows), rows)
    for i, (start, size) in enumerate(pieces):
        total = parts[i, at, :]
        for k in range(chips):
            total = total + red_in[k, :, start : start + size].astype(F32)
        hgrad_ref[:, start : start + size] = total.astype(BF16)

    for i in range(chips - 1):
        hidden_out(i).wait_send()
        reduce_to(i, 0).wait_send()
        reduce_to(i, 1).wait_send()
    for i in range(chips):
        forward(i).wait_send()
    for i in range(n - 1):
        teacher_out(i).wait_send()
        stat_to(i).wait_send()
    for i in range(len(pieces)):
        pair(i).wait_send()


def out_kernel(div, hgrad, wgrad, div_out, hgrad_out, wgrad_out, sem):
    strip = wgrad.shape[0] // 8
    copies = [
        pltpu.make_async_copy(wgrad.at[pl.ds(i * strip, strip)], wgrad_out.at[pl.ds(i * strip, strip)], sem.at[i])
        for i in range(8)
    ]
    copies.append(pltpu.make_async_copy(div, div_out, sem.at[8]))
    copies.append(pltpu.make_async_copy(hgrad, hgrad_out, sem.at[9]))
    for copy in copies:
        copy.start()
    for copy in copies:
        copy.wait()


def on_device(hidden, head_weight, teacher_logits, token_ids, teacher_map, student_map):
    n = lax.axis_size("voc")
    chips = n // 2
    rows, width = hidden.shape
    block = head_weight.shape[1]
    tokens = n * rows
    half = chips * rows
    pieces = len(tiles(width, 256))
    dma = pltpu.SemaphoreType.DMA
    vmem = pl.BlockSpec(memory_space=pltpu.VMEM)
    hbm = pl.BlockSpec(memory_space=pltpu.HBM)
    div, hgrad, wgrad = pl.pallas_call(
        functools.partial(kernel, n),
        out_shape=(
            pltpu.VMEM((1, tokens), F32),
            pltpu.VMEM((rows, width), BF16),
            pltpu.VMEM((width, block), BF16),
        ),
        in_specs=[hbm] * 6,
        out_specs=(vmem, vmem, vmem),
        scratch_shapes=[
            pltpu.VMEM((1, tokens), jnp.int32),
            pltpu.SMEM((n,), jnp.int32),
            pltpu.SMEM((n,), jnp.int32),
            pltpu.VMEM((width, block), BF16),
            pltpu.VMEM((n, rows, block), BF16),
            pltpu.VMEM((n, rows, block), BF16),
            pltpu.VMEM((n, rows, block), BF16),
            pltpu.VMEM((n, rows, width), BF16),
            pltpu.VMEM((tokens, width), BF16),
            pltpu.VMEM((width, tokens), BF16),
            pltpu.VMEM((tokens, block), BF16),
            pltpu.VMEM((block, width), BF16),
            pltpu.VMEM((tokens, block), F32),
            pltpu.VMEM((tokens, block), F32),
            pltpu.VMEM((tokens, 128), F32),
            pltpu.VMEM((tokens, 128), F32),
            pltpu.VMEM((tokens, 128), F32),
            pltpu.VMEM((tokens, 128), F32),
            pltpu.VMEM((tokens, 128), F32),
            pltpu.VMEM((tokens, 128), F32),
            pltpu.VMEM((tokens, 128), F32),
            pltpu.VMEM((4, tokens), F32),
            pltpu.VMEM((n, 4, tokens), F32),
            pltpu.VMEM((pieces, tokens, 256), F32),
            pltpu.VMEM((pieces, half, 256), F32),
            pltpu.VMEM((chips, rows, width), BF16),
            pltpu.VMEM((chips, rows, width), BF16),
            dma((5,)),
            dma((n,)),
            dma((n,)),
            dma((n,)),
            dma((chips,)),
            dma((chips,)),
            dma((chips,)),
            dma((chips,)),
            dma((n,)),
            dma((n,)),
            dma((pieces,)),
            dma((pieces,)),
            dma((2, chips)),
            dma((2, chips)),
        ],
        compiler_params=pltpu.CompilerParams(
            collective_id=0, has_side_effects=True, vmem_limit_bytes=48 * 1024 * 1024
        ),
    )(*(
        pltpu.with_memory_space_constraint(x, pltpu.HBM)
        for x in (hidden, head_weight, teacher_logits, token_ids.reshape(1, tokens), teacher_map, student_map)
    ))
    div, hgrad, wgrad = pl.pallas_call(
        out_kernel,
        out_shape=(
            jax.ShapeDtypeStruct((1, tokens), F32),
            jax.ShapeDtypeStruct((rows, width), BF16),
            jax.ShapeDtypeStruct((width, block), BF16),
        ),
        in_specs=[vmem] * 3,
        out_specs=(hbm,) * 3,
        scratch_shapes=[dma((10,))],
        compiler_params=pltpu.CompilerParams(vmem_limit_bytes=2 * 1024 * 1024),
    )(*(pltpu.with_memory_space_constraint(x, pltpu.VMEM) for x in (div, hgrad, wgrad)))
    return div.reshape(tokens), hgrad, wgrad


def solution(mesh):
    return jax.shard_map(
        on_device,
        mesh=mesh,
        in_specs=(
            P(("grp", "voc"), None),
            P(None, "voc"),
            P(("grp", "voc"), None),
            P("grp"),
            P(),
            P(),
        ),
        out_specs=(P("grp"), P(("grp", "voc"), None), P(None, ("grp", "voc"))),
        check_vma=False,
    )
```
